512 devices in a mesh: rows: 32 (over z, y_hi), samp: 16 (over x, y_lo, core).
Axes of the slice: x: 4, y: 4 (y_hi: 2, y_lo: 2; y = y_hi * 2 + y_lo), z: 16, core: 2. Of those that a mesh axis runs over, the one named last changes fastest.
Arguments:
- atom_noised: bfloat16 [48, 16384, 128], P('samp', 'rows'), may hold values from -6 to 6
- atom_single: bfloat16 [16384, 128], P('rows'), may hold values from -6 to 6
- atom_token: int32 [16384], P('rows'), may hold values from 0 to 2047, as said below
- atom_count: int32 [32], P('rows'), may hold values from 320 to 512, as said below
- token_single: bfloat16 [2048, 768], P('rows')
- pair_bias: bfloat16 [8, 2048, 2048], P(None, 'rows'), may hold values from -4 to 350
- w_atom: bfloat16 [128, 128], replicated, may hold values from -0.5 to 0.5
- w_up: bfloat16 [128, 768], P('samp'), may hold values from -0.5 to 0.5
- w_query: bfloat16 [768, 384], P('samp'), may hold values from -0.21875 to 0.21875
- w_key: bfloat16 [768, 384], P('samp'), may hold values from -0.21875 to 0.21875
- w_value: bfloat16 [768, 384], P('samp'), may hold values from -0.21875 to 0.21875
- w_out: bfloat16 [384, 768], P('samp'), may hold values from -0.3125 to 0.3125
- w_down: bfloat16 [768, 128], P('samp'), may hold values from -0.21875 to 0.21875
- d_atom_out: bfloat16 [48, 16384, 128], P('samp', 'rows'), may hold values from -6 to 6
Outputs:
- atom_out: bfloat16 [48, 16384, 128], P('samp', 'rows')
- bias_grad: float32 [8, 2048, 2048], P(None, 'rows', 'samp')
The draws below stay inside these ranges and needn't reach their ends.
Inputs may be any that keep to these rules, and one draw needn't show every extreme that they name: Index r of rows holds the slots r * 512 to (r + 1) * 512 - 1; its first atom_count[r] slots are atoms, the rest padding. Some index is full in every draw. `atom_token`: A slot of index r of rows names a token between r * 64 - 32 and (r + 1) * 64 + 31; along one index's slots the tokens never fall. Padding slots name tokens too.
All inputs are finite; a program needn't handle non-finite values.
Results may differ from the reference program's by a relative error of at most 0.04.
Values may be sent and summed in bfloat16 or wider, within the bound.
No kernel may reach another device: no remote copies, remote signals or barrier semaphores. Data moves between devices by JAX's collectives and lax.ppermute only.
A program may use at most 128 MiB of HBM per device.

```python
import jax
import jax.numpy as jnp
from jax import lax

D = 768
CA = 128
HEADS = 8
HEAD_DIM = 48
TOK_DEV = 64
S_DEV = 3
INNER = 384
ATOM_DEV = 512
MARGIN = 32
TOKENS = 2048
ATOMS = 16384
SAMPLES = 48
N_ROWS = 32
N_SAMP = 16


def draw_atom_count(key, part):
    key = jax.random.fold_in(key, 11)
    first_key, second_key = jax.random.split(key)
    counts = jax.random.randint(first_key, (N_ROWS,), ATOM_DEV * 5 // 8, ATOM_DEV + 1)
    chosen = jax.random.randint(second_key, (), 0, N_ROWS)
    filled = jnp.where(jnp.arange(N_ROWS) == chosen, ATOM_DEV, counts)
    return filled.astype(jnp.int32)


def draw_atom_token(key, part):
    key = jax.random.fold_in(key, 12)
    raw_slots = jax.random.randint(key, (N_ROWS, ATOM_DEV), 0, 2 * TOK_DEV)
    column = jnp.arange(ATOM_DEV)[None, :]
    raw_slots = jnp.where(column == 0, 0, jnp.where(column == ATOM_DEV - 1, 2 * TOK_DEV - 1, raw_slots))
    ordered = jnp.sort(raw_slots, axis=1)
    offsets = jnp.arange(N_ROWS)[:, None] * TOK_DEV - MARGIN
    return jnp.clip(offsets + ordered, 0, TOKENS - 1).reshape(-1).astype(jnp.int32)


def draw_token_single(key, part):
    key = jax.random.fold_in(key, 13)
    base_key, row_key, col_key = jax.random.split(key, 3)
    row_scale = jnp.exp(jax.random.uniform(row_key, (TOKENS, 1), jnp.float32, jnp.log(0.3), jnp.log(3.0)))
    col_scale = jnp.exp(jax.random.uniform(col_key, (1, D), jnp.float32, jnp.log(0.3), jnp.log(3.0)))
    base = jnp.clip(jax.random.normal(base_key, (TOKENS, D), jnp.float32), -6.0, 6.0)
    return (base * row_scale * col_scale).astype(jnp.bfloat16)


def draw_pair_bias(key, part):
    key = jax.random.fold_in(key, 14)
    base = jnp.clip(jax.random.normal(key, (HEADS, TOKENS, TOKENS), jnp.float32), -4.0, 4.0)
    return base.astype(jnp.bfloat16)


def shard_levels(own_key, shape, pieces, smallest, high):
    factor_of = 1.0
    for dim, shards_of in pieces:
        steps = jax.random.uniform(jax.random.fold_in(jax.random.fold_in(own_key, 6), dim), (shards_of,), jnp.float32, smallest / len(pieces), high / len(pieces))
        factor_of = factor_of * jnp.repeat(jnp.exp(steps), shape[dim] // shards_of).reshape((-1,) + (1,) * (len(shape) - 1 - dim))
    return factor_of


def noise(stream_key, dims, width, reach, shards=(), held_as=jnp.bfloat16):
    gain = shard_levels(stream_key, dims, shards, -0.22, 0.18) if shards else 1.0
    result = jax.random.normal(stream_key, dims, jnp.float32) * width * gain
    return jnp.minimum(jnp.maximum(result, -reach), reach).astype(held_as)


def setup_inputs(seed: int = 0) -> dict:
    splits = jax.random.split(jax.random.key(seed), 15)
    atom_noised = noise(splits[0], (SAMPLES, ATOMS, CA), 1.0, 6.0, ((0, 16), (1, 32)))
    atom_single = noise(splits[1], (ATOMS, CA), 1.0, 6.0, ((0, 32),))
    atom_token = draw_atom_token(jax.random.fold_in(splits[14], 71), 0)
    atom_count = draw_atom_count(jax.random.fold_in(splits[14], 71), 0)
    token_single = draw_token_single(jax.random.fold_in(splits[14], 71), 0)
    pair_bias = draw_pair_bias(jax.random.fold_in(splits[14], 71), 0)
    w_atom = noise(splits[6], (CA, CA), CA ** -0.5, 0.5)
    w_up = noise(splits[7], (CA, D), CA ** -0.5, 0.5, ((0, 16),))
    w_query = noise(splits[8], (D, INNER), D ** -0.5, 0.21875, ((0, 16),))
    w_key = noise(splits[9], (D, INNER), D ** -0.5, 0.21875, ((0, 16),))
    w_value = noise(splits[10], (D, INNER), D ** -0.5, 0.21875, ((0, 16),))
    w_out = noise(splits[11], (INNER, D), INNER ** -0.5, 0.3125, ((0, 16),))
    w_down = noise(splits[12], (D, CA), D ** -0.5, 0.21875, ((0, 16),))
    d_atom_out = noise(splits[13], (SAMPLES, ATOMS, CA), 1.0, 6.0, ((0, 16), (1, 32)))
    return dict(atom_noised=atom_noised, atom_single=atom_single, atom_token=atom_token, atom_count=atom_count, token_single=token_single, pair_bias=pair_bias, w_atom=w_atom, w_up=w_up, w_query=w_query, w_key=w_key, w_value=w_value, w_out=w_out, w_down=w_down, d_atom_out=d_atom_out)


EPSILON = 1e-05

def normalize(values):
    average = lax.optimization_barrier(jnp.mean(values, axis=-1, keepdims=True))
    centered = values - average
    variance = lax.optimization_barrier(jnp.mean(centered * centered, axis=-1, keepdims=True))
    inverse = lax.rsqrt(variance + EPSILON)
    return (centered * inverse, inverse)

def product(left, right, form):
    return jnp.einsum(form, left.astype(jnp.float32), right.astype(jnp.float32))

def reference(atom_noised, atom_single, atom_token, atom_count, token_single, pair_bias, w_atom, w_up, w_query, w_key, w_value, w_out, w_down, d_atom_out):
    slot_index = jnp.arange(ATOMS, dtype=jnp.int32)
    owner_rank = slot_index // ATOM_DEV
    living = (slot_index % ATOM_DEV < atom_count[owner_rank]).astype(jnp.float32)

    def pool_atoms(values):
        weighted = jnp.moveaxis(values.astype(jnp.float32) * living[None, :, None], 1, 0)
        summed = jax.ops.segment_sum(weighted, atom_token, num_segments=TOKENS)
        return jnp.moveaxis(summed, 0, 1)
    atom_query = (atom_noised.astype(jnp.float32) + atom_single.astype(jnp.float32)[None]).astype(jnp.bfloat16)
    hidden_pre = product(atom_query, w_atom, 'sac,cd->sad')
    atom_hidden = (atom_query.astype(jnp.float32) + jax.nn.silu(hidden_pre)).astype(jnp.bfloat16)
    counts = jax.ops.segment_sum(living, atom_token, num_segments=TOKENS)
    pooled = (pool_atoms(atom_hidden) / jnp.maximum(counts, 1.0)[None, :, None]).astype(jnp.bfloat16)
    tokens_in = product(pooled, w_up, 'stc,cd->std') + token_single.astype(jnp.float32)[None]
    normed, _ = normalize(tokens_in)
    normed_b = normed.astype(jnp.bfloat16)
    scaling = HEAD_DIM ** (-0.5)
    queries = (product(normed_b, w_query, 'std,de->ste') * scaling).astype(jnp.bfloat16)
    keys_tok = product(normed_b, w_key, 'std,de->ste').astype(jnp.bfloat16)
    values_tok = product(normed_b, w_value, 'std,de->ste').astype(jnp.bfloat16)
    split_shape = (SAMPLES, TOKENS, HEADS, HEAD_DIM)
    queries = queries.reshape(split_shape)
    keys_tok = keys_tok.reshape(split_shape)
    values_tok = values_tok.reshape(split_shape)
    bias_full = pair_bias.astype(jnp.float32)

    def softmax_rows(query_s, key_s):
        scores = product(query_s, key_s, 'ihe,jhe->hij') + bias_full
        return jax.nn.softmax(scores, axis=-1)

    def attend(operands):
        query_s, key_s, value_s = operands
        prob_rows = softmax_rows(query_s, key_s)
        return product(prob_rows.astype(jnp.bfloat16), value_s, 'hij,jhe->ihe').astype(jnp.bfloat16)
    mixed = lax.map(attend, (queries, keys_tok, values_tok)).reshape(SAMPLES, TOKENS, INNER)
    tokens_out = tokens_in + product(mixed, w_out, 'ste,ed->std')
    normed_out, inverse_out = normalize(tokens_out)
    token_proj = product(normed_out.astype(jnp.bfloat16), w_down, 'std,dc->stc').astype(jnp.bfloat16)
    picked = jnp.take(token_proj, atom_token, axis=1).astype(jnp.float32)
    atom_out = (living[None, :, None] * (atom_hidden.astype(jnp.float32) + picked)).astype(jnp.bfloat16)
    d_token = pool_atoms(d_atom_out).astype(jnp.bfloat16)
    d_normed = product(d_token, w_down, 'stc,dc->std')
    first_term = lax.optimization_barrier(jnp.mean(d_normed, axis=-1, keepdims=True))
    second_term = lax.optimization_barrier(jnp.mean(d_normed * normed_out, axis=-1, keepdims=True))
    d_tokens = inverse_out * (d_normed - first_term - normed_out * second_term)
    d_mixed = product(d_tokens.astype(jnp.bfloat16), w_out, 'std,ed->ste').astype(jnp.bfloat16)
    d_mixed = d_mixed.reshape(split_shape)
    group_shape = (N_SAMP, S_DEV, TOKENS, HEADS, HEAD_DIM)
    factor = TOKENS / SAMPLES

    def sample_step(carry, operands):
        query_s, key_s, value_s, dmix_s = operands
        prob_rows = softmax_rows(query_s, key_s)
        d_probs = product(dmix_s, value_s, 'ihe,jhe->hij')
        delta = lax.optimization_barrier(jnp.sum(prob_rows * d_probs, axis=-1, keepdims=True))
        return (carry + prob_rows * (d_probs - delta), None)

    def group_step(total, operands):
        start = jnp.zeros((HEADS, TOKENS, TOKENS), jnp.float32)
        summed, _ = lax.scan(sample_step, start, operands)
        rounded = (summed * factor).astype(jnp.bfloat16)
        rounded = lax.optimization_barrier(rounded)
        return (total + rounded.astype(jnp.float32), None)
    grouped = (queries.reshape(group_shape), keys_tok.reshape(group_shape), values_tok.reshape(group_shape), d_mixed.reshape(group_shape))
    bias_grad, _ = lax.scan(group_step, jnp.zeros((HEADS, TOKENS, TOKENS), jnp.float32), grouped)
    return (atom_out, bias_grad)
```

```python
import functools

import jax
import jax.numpy as jnp
from jax import lax
from jax.experimental import pallas as pl
from jax.experimental.pallas import tpu as pltpu
from jax.sharding import PartitionSpec as P

EPSILON = 1e-05
F32 = jnp.float32
BF16 = jnp.bfloat16
VMEM_BYTES = 56 * 1024 * 1024
WHOLE = pl.BlockSpec(memory_space=pltpu.VMEM)
SCALAR = pl.BlockSpec(memory_space=pltpu.SMEM)
ANY = pl.BlockSpec(memory_space=pl.ANY)


def dot(left, right):
    return lax.dot_general(left, right, (((1,), (0,)), ((), ())), preferred_element_type=F32)


def dot_nt(left, right):
    return lax.dot_general(left, right, (((1,), (1,)), ((), ())), preferred_element_type=F32)


def params():
    return pltpu.CompilerParams(vmem_limit_bytes=VMEM_BYTES)


def normalize(values):
    average = jnp.mean(values, axis=-1, keepdims=True)
    centered = values - average
    variance = jnp.mean(centered * centered, axis=-1, keepdims=True)
    inverse = lax.rsqrt(variance + EPSILON)
    return centered * inverse, inverse


def pool_kernel(count, token, noised, single, w_atom, d_out, hidden, own, left, right):
    samples, atoms, channels = noised.shape
    wide = own.shape[1] + left.shape[1] + right.shape[1]
    margin = left.shape[1]
    middle = own.shape[1]
    slot = lax.broadcasted_iota(jnp.int32, (wide, atoms), 1)
    line = lax.broadcasted_iota(jnp.int32, (wide, atoms), 0)
    picked = (line == token[...]) & (slot < count[0])
    one_hot = jnp.where(picked, 1.0, 0.0).astype(BF16)

    def put(index, sums):
        left[index] = sums[:margin]
        own[index] = sums[margin : margin + middle]
        right[index] = sums[margin + middle :]

    single_f = single[...].astype(F32)
    for s in range(samples):
        query = (noised[s].astype(F32) + single_f).astype(BF16)
        pre = dot(query, w_atom[...])
        value = (query.astype(F32) + pre / (1.0 + jnp.exp(-pre))).astype(BF16)
        hidden[s] = value
        put(s, dot(one_hot, value))
    put(samples, dot(one_hot, jnp.ones((atoms, channels), BF16)))
    for s in range(samples):
        put(samples + 1 + s, dot(one_hot, d_out[s]))


def settle_kernel(own, from_left, from_right, pooled, d_token):
    margin = from_left.shape[1]
    samples = (own.shape[0] - 1) // 2
    middle = own.shape[1]

    def settled(index):
        return jnp.concatenate(
            [own[index, :margin] + from_left[index], own[index, margin:] + from_right[index]], axis=0
        )

    scale = 1.0 / jnp.maximum(settled(samples), 1.0)
    for s in range(samples):
        pooled[s * middle : (s + 1) * middle] = (settled(s) * scale).astype(BF16)
        d_token[s * middle : (s + 1) * middle] = settled(samples + 1 + s).astype(BF16)


def prep_kernel(inner, t_ref, w_up, w_all, t_cent, base, w_cent, w_kv):
    @pl.when(pl.program_id(0) == 0)
    def _():
        up = w_up[...].astype(F32)
        cent = (up - jnp.mean(up, axis=-1, keepdims=True)).astype(BF16)
        w_cent[...] = cent
        w_kv[...] = dot(cent, w_all[:, inner : 3 * inner]).astype(BF16)

    t = t_ref[...].astype(F32)
    cent = (t - jnp.mean(t, axis=-1, keepdims=True)).astype(BF16)
    t_cent[...] = cent
    base[...] = dot(cent, w_all[:, inner : 3 * inner])


def attend_kernel(
    heads,
    factor,
    place,
    pooled_all,
    t_cent,
    base,
    w_cent,
    w_kv,
    pooled,
    t_own,
    w_up,
    w_all,
    w_out,
    bias_hbm,
    d_token,
    proj,
    keep,
    send,
    t_blk,
    base_blk,
    bias,
    kv,
    tokens_in,
    queries,
    scores,
    probs,
    mixed_full,
    inv_sum,
    mixed,
    d_mixed,
    t_sem,
    base_sem,
    bias_sem,
):
    blocks, samples, tok, channels = pooled_all.shape
    pairs = blocks // 2
    block = 2 * tok
    total = blocks * tok
    width = t_own.shape[1]
    inner = w_out.shape[0]
    head_dim = inner // heads
    half = heads // 2
    rows = half * tok
    span = 256
    starts = (0, inner - span)
    rank = place[0]
    core = place[1]

    def fetch(b):
        slot = lax.rem(b, 2)
        where = pl.ds(pl.multiple_of(b * block, block), block)
        return (
            pltpu.make_async_copy(t_cent.at[where], t_blk.at[slot], t_sem.at[slot]),
            pltpu.make_async_copy(base.at[where], base_blk.at[slot], base_sem.at[slot]),
        )

    bias_copy = pltpu.make_async_copy(bias_hbm, bias, bias_sem)
    for copy in fetch(0):
        copy.start()
    bias_copy.start()

    t_f = t_own[...].astype(F32)
    for s in range(samples):
        own_rows = slice(s * tok, (s + 1) * tok)
        tokens_in[own_rows] = dot(pooled[own_rows], w_up[...]) + t_f
    normed, _ = normalize(tokens_in[...])
    queries[...] = (dot(normed.astype(BF16), w_all[:, :inner]) * (head_dim**-0.5)).astype(BF16)

    def kv_step(b, carry):
        slot = lax.rem(b, 2)

        @pl.when(b + 1 < pairs)
        def _():
            for copy in fetch(b + 1):
                copy.start()

        for copy in fetch(b):
            copy.wait()
        owner = [lax.rem(rank + 2 * b + part, blocks) for part in range(2)]
        p = jnp.concatenate([pooled_all[o, s] for s in range(samples) for o in owner], axis=0)
        x = dot(p, w_cent[...])
        y = dot(p, w_kv[...])
        tb = t_blk[slot].astype(F32)
        bb = base_blk[slot]
        for s in range(samples):
            part = slice(s * block, (s + 1) * block)
            centered = x[part] + tb
            inverse = lax.rsqrt(jnp.sum(centered * centered, axis=-1, keepdims=True) / width + EPSILON)
            result = ((y[part] + bb) * inverse).astype(BF16)
            for i, o in enumerate(owner):
                kv[s, pl.ds(pl.multiple_of(o * tok, tok), tok), :] = result[i * tok : (i + 1) * tok]
        return carry

    lax.fori_loop(0, pairs, kv_step, 0)
    bias_copy.wait()

    lane_head = lax.broadcasted_iota(jnp.int32, (rows, span), 1)
    row_head = lax.broadcasted_iota(jnp.int32, (rows, span), 0) // tok

    def head_mask(g):
        lo = (row_head + g * half) * head_dim - starts[g]
        return (lane_head >= lo) & (lane_head < lo + head_dim)

    def spread(values, g):
        tile = values[:, starts[g] : starts[g] + span].astype(F32)
        return jnp.where(head_mask(g), jnp.concatenate([tile] * half, axis=0), 0.0)

    chunk = 512

    def forward(s, carry):
        own_rows = pl.ds(pl.multiple_of(s * tok, tok), tok)
        pieces = []
        for g in range(2):
            q = spread(queries[own_rows, :], g).astype(BF16)
            lanes = slice(starts[g], starts[g] + span)
            value_lanes = slice(inner + starts[g], inner + starts[g] + span)
            top = jnp.full((rows, 128), -jnp.inf, F32)
            for j in range(0, total, chunk):
                part = dot_nt(q, kv[s, j : j + chunk, lanes])
                part = part + bias[g * rows : (g + 1) * rows, j : j + chunk].astype(F32)
                scores[g, :, j : j + chunk] = part
                for c in range(0, chunk, 128):
                    top = jnp.maximum(top, part[:, c : c + 128])
            top = jnp.max(top, axis=-1, keepdims=True)
            amount = jnp.zeros((rows, 128), F32)
            out = jnp.zeros((rows, span), F32)
            for j in range(0, total, chunk):
                e = jnp.exp(scores[g, :, j : j + chunk] - top)
                for c in range(0, chunk, 128):
                    amount = amount + e[:, c : c + 128]
                e = e.astype(BF16)
                probs[s, g, :, j : j + chunk] = e
                out = out + dot(e, kv[s, j : j + chunk, value_lanes])
            inverse = 1.0 / jnp.sum(amount, axis=-1, keepdims=True)
            out = jnp.where(head_mask(g), out * inverse, 0.0)
            mixed_full[s, g] = out
            inv_sum[s, g] = jnp.broadcast_to(inverse, (rows, 128))
            piece = out[:tok]
            for h in range(1, half):
                piece = piece + out[h * tok : (h + 1) * tok]
            pieces.append(piece)
        cut = starts[1]
        mixed[own_rows, :cut] = pieces[0][:, :cut].astype(BF16)
        mixed[own_rows, cut:span] = (pieces[0][:, cut:] + pieces[1][:, : span - cut]).astype(BF16)
        mixed[own_rows, span:] = pieces[1][:, span - cut :].astype(BF16)
        return carry

    lax.fori_loop(0, samples, forward, 0)

    w_down = w_all[:, 3 * inner :]
    normed_out, inverse_out = normalize(tokens_in[...] + dot(mixed[...], w_out[...]))
    proj[...] = dot(normed_out.astype(BF16), w_down).astype(BF16)
    d_normed = dot_nt(d_token[...], w_down)
    first = jnp.mean(d_normed, axis=-1, keepdims=True)
    second = jnp.mean(d_normed * normed_out, axis=-1, keepdims=True)
    d_tokens = inverse_out * (d_normed - first - normed_out * second)
    d_mixed[...] = dot_nt(d_tokens.astype(BF16), w_out[...]).astype(BF16)

    for g in range(2):
        value_lanes = slice(inner + starts[g], inner + starts[g] + span)
        wide = []
        delta = []
        scale = []
        for s in range(samples):
            w = spread(d_mixed[s * tok : (s + 1) * tok, :], g)
            wide.append(w.astype(BF16))
            delta.append(jnp.sum(w * mixed_full[s, g], axis=-1, keepdims=True))
            scale.append(inv_sum[s, g][:, :1] * factor)

        def backward(k, carry):
            cols = pl.ds(pl.multiple_of(k * 256, 256), 256)
            grad = None
            for s in range(samples):
                d_prob = dot_nt(wide[s], kv[s, cols, value_lanes])
                term = probs[s, g, :, cols].astype(F32) * ((d_prob - delta[s]) * scale[s])
                grad = term if grad is None else grad + term
            low = grad[:, :128]
            high = grad[:, 128:]
            keep[k, g * rows : (g + 1) * rows, :] = jnp.where(core == 0, low, high).astype(BF16)
            send[k, g * rows : (g + 1) * rows, :] = jnp.where(core == 0, high, low).astype(BF16)
            return carry

        lax.fori_loop(0, total // 256, backward, 0)


def decode_kernel(count, token, hidden, proj, from_left, from_right, out):
    samples, atoms, channels = hidden.shape
    tok = proj.shape[1]
    wide = tok + 2 * from_left.shape[1]
    line = lax.broadcasted_iota(jnp.int32, (atoms, wide), 1)
    one_hot = jnp.where(line == token[...], 1.0, 0.0).astype(BF16)
    alive = lax.broadcasted_iota(jnp.int32, (atoms, channels), 0) < count[0]
    for s in range(samples):
        table = jnp.concatenate([from_left[s], proj[s], from_right[s]], axis=0)
        value = hidden[s].astype(F32) + dot(one_hot, table)
        out[s] = jnp.where(alive, value, 0.0).astype(BF16)


def local(
    atom_noised,
    atom_single,
    atom_token,
    atom_count,
    token_single,
    pair_bias,
    w_atom,
    w_up,
    w_query,
    w_key,
    w_value,
    w_out,
    w_down,
    d_atom_out,
):
    samples, atoms, channels = atom_noised.shape
    tok, width = token_single.shape
    margin = tok // 2
    heads, _, total = pair_bias.shape
    n_rows = lax.axis_size("rows")
    n_samp = lax.axis_size("samp")
    inner = w_query.shape[1]
    rank = lax.axis_index("rows")
    group = lax.axis_index("samp")
    chips = n_samp // 2

    fetched = []
    for part in range(2):
        perm = [
            ((r + 2 * s + part) % n_rows * n_samp + s, r * n_samp + s)
            for r in range(n_rows)
            for s in range(n_samp)
        ]
        fetched.append(lax.ppermute(token_single, ("rows", "samp"), perm))

    local_token = atom_token - (rank * tok - margin)
    shape = jax.ShapeDtypeStruct
    sums = 2 * samples + 1
    hidden, own, left, right = pl.pallas_call(
        pool_kernel,
        out_shape=(
            shape((samples, atoms, channels), BF16),
            shape((sums, tok, channels), F32),
            shape((sums, margin, channels), F32),
            shape((sums, margin, channels), F32),
        ),
        in_specs=[SCALAR] + [WHOLE] * 5,
        out_specs=(WHOLE,) * 4,
        compiler_params=params(),
        name="pool",
    )(atom_count, local_token[None, :], atom_noised, atom_single, w_atom, d_atom_out)
    up = [(i, i + 1) for i in range(n_rows - 1)]
    down = [(i + 1, i) for i in range(n_rows - 1)]
    from_left = lax.ppermute(right, "rows", up)
    from_right = lax.ppermute(left, "rows", down)
    pooled, d_token = pl.pallas_call(
        settle_kernel,
        out_shape=(shape((samples * tok, channels), BF16), shape((samples * tok, channels), BF16)),
        in_specs=[WHOLE] * 3,
        out_specs=(WHOLE,) * 2,
        compiler_params=params(),
        name="settle",
    )(own, from_left, from_right)
    pooled_all = lax.all_gather(pooled, "rows", axis=0, tiled=True)
    pooled_all = pooled_all.reshape(n_rows, samples, tok, channels)

    w_all = lax.all_gather(
        jnp.concatenate([w_query, w_key, w_value, w_down], axis=1), "samp", axis=0, tiled=True
    )
    w_two = lax.all_gather(jnp.concatenate([w_up, w_out], axis=0), "samp", axis=0, tiled=False)
    w_up_all = w_two[:, : w_up.shape[0]].reshape(-1, width)
    w_out_all = w_two[:, w_up.shape[0] :].reshape(-1, width)
    t_all = lax.all_gather(jnp.concatenate(fetched, axis=0), "samp", axis=0, tiled=True)

    block = 256
    t_cent, base, w_cent, w_kv = pl.pallas_call(
        functools.partial(prep_kernel, inner),
        grid=(total // block,),
        out_shape=(
            shape((total, width), BF16),
            shape((total, 2 * inner), F32),
            shape((channels, width), BF16),
            shape((channels, 2 * inner), BF16),
        ),
        in_specs=[
            pl.BlockSpec((block, width), lambda i: (i, 0)),
            pl.BlockSpec((channels, width), lambda i: (0, 0)),
            pl.BlockSpec(w_all.shape, lambda i: (0, 0)),
        ],
        out_specs=(
            pl.BlockSpec((block, width), lambda i: (i, 0)),
            pl.BlockSpec((block, 2 * inner), lambda i: (i, 0)),
            pl.BlockSpec((channels, width), lambda i: (0, 0)),
            pl.BlockSpec((channels, 2 * inner), lambda i: (0, 0)),
        ),
        compiler_params=params(),
        name="prep",
    )(t_all, w_up_all, w_all)

    place = jnp.stack([rank, group % 2]).astype(jnp.int32)
    factor = total / (samples * n_samp)
    rows = heads // 2 * tok
    proj, keep, send = pl.pallas_call(
        functools.partial(attend_kernel, heads, factor),
        out_shape=(
            shape((samples * tok, channels), BF16),
            shape((chips, heads * tok, 128), BF16),
            shape((chips, heads * tok, 128), BF16),
        ),
        in_specs=[SCALAR, WHOLE, ANY, ANY] + [WHOLE] * 7 + [ANY, WHOLE],
        out_specs=(WHOLE,) * 3,
        scratch_shapes=[
            pltpu.VMEM((2, 2 * tok, width), BF16),
            pltpu.VMEM((2, 2 * tok, 2 * inner), F32),
            pltpu.VMEM((heads * tok, total), BF16),
            pltpu.VMEM((samples, total, 2 * inner), BF16),
            pltpu.VMEM((samples * tok, width), F32),
            pltpu.VMEM((samples * tok, inner), BF16),
            pltpu.VMEM((2, rows, total), F32),
            pltpu.VMEM((samples, 2, rows, total), BF16),
            pltpu.VMEM((samples, 2, rows, 256), F32),
            pltpu.VMEM((samples, 2, rows, 128), F32),
            pltpu.VMEM((samples * tok, inner), BF16),
            pltpu.VMEM((samples * tok, inner), BF16),
            pltpu.SemaphoreType.DMA((2,)),
            pltpu.SemaphoreType.DMA((2,)),
            pltpu.SemaphoreType.DMA,
        ],
        compiler_params=params(),
        name="attend",
    )(
        place,
        pooled_all,
        t_cent,
        base,
        w_cent,
        w_kv,
        pooled,
        token_single,
        w_up_all,
        w_all,
        w_out_all,
        pair_bias.reshape(heads * tok, total),
        d_token,
    )

    swap = [(s, s ^ 1) for s in range(n_samp)]
    other = lax.ppermute(send, "samp", swap)
    both = (keep.astype(F32) + other.astype(F32)).astype(BF16)
    sets = [[2 * m + c for m in range(chips)] for c in range(2)]
    shares = lax.all_to_all(both, "samp", 0, 0, axis_index_groups=sets, tiled=True)
    bias_grad = jnp.sum(shares.astype(F32), axis=0).reshape(heads, tok, 128)

    proj = proj.reshape(samples, tok, channels)
    proj_left = lax.ppermute(proj[:, margin:], "rows", up)
    proj_right = lax.ppermute(proj[:, :margin], "rows", down)
    atom_out = pl.pallas_call(
        decode_kernel,
        out_shape=shape((samples, atoms, channels), BF16),
        in_specs=[SCALAR] + [WHOLE] * 5,
        out_specs=WHOLE,
        compiler_params=params(),
        name="decode",
    )(atom_count, local_token[:, None], hidden, proj, proj_left, proj_right)
    return (atom_out, bias_grad)


def solution(mesh):
    placed = (
        P("samp", "rows", None),
        P("rows", None),
        P("rows"),
        P("rows"),
        P("rows", None),
        P(None, "rows", None),
        P(),
        P("samp", None),
        P("samp", None),
        P("samp", None),
        P("samp", None),
        P("samp", None),
        P("samp", None),
        P("samp", "rows", None),
    )
    return jax.shard_map(
        local,
        mesh=mesh,
        in_specs=placed,
        out_specs=(P("samp", "rows", None), P(None, "rows", "samp")),
        check_vma=False,
    )
```

```python
import functools

import jax
import jax.numpy as jnp
from jax import lax
from jax.experimental import pallas as pl
from jax.experimental.pallas import tpu as pltpu
from jax.sharding import PartitionSpec as P

EPSILON = 1e-05
F32 = jnp.float32
BF16 = jnp.bfloat16
VMEM_BYTES = 56 * 1024 * 1024
WHOLE = pl.BlockSpec(memory_space=pltpu.VMEM)
SCALAR = pl.BlockSpec(memory_space=pltpu.SMEM)
ANY = pl.BlockSpec(memory_space=pl.ANY)


def dot(left, right):
    return lax.dot_general(left, right, (((1,), (0,)), ((), ())), preferred_element_type=F32)


def dot_nt(left, right):
    return lax.dot_general(left, right, (((1,), (1,)), ((), ())), preferred_element_type=F32)


def params():
    return pltpu.CompilerParams(vmem_limit_bytes=VMEM_BYTES)


def normalize(values):
    average = jnp.mean(values, axis=-1, keepdims=True)
    centered = values - average
    variance = jnp.mean(centered * centered, axis=-1, keepdims=True)
    inverse = lax.rsqrt(variance + EPSILON)
    return centered * inverse, inverse


def pool_kernel(count, token, noised, single, w_atom, d_out, hidden, own, left, right):
    samples, atoms, channels = noised.shape
    wide = own.shape[1] + left.shape[1] + right.shape[1]
    margin = left.shape[1]
    middle = own.shape[1]
    slot = lax.broadcasted_iota(jnp.int32, (wide, atoms), 1)
    line = lax.broadcasted_iota(jnp.int32, (wide, atoms), 0)
    picked = (line == token[...]) & (slot < count[0])
    one_hot = jnp.where(picked, 1.0, 0.0).astype(BF16)

    def put(index, sums):
        left[index] = sums[:margin]
        own[index] = sums[margin : margin + middle]
        right[index] = sums[margin + middle :]

    single_f = single[...].astype(F32)
    for s in range(samples):
        query = (noised[s].astype(F32) + single_f).astype(BF16)
        pre = dot(query, w_atom[...])
        value = (query.astype(F32) + pre / (1.0 + jnp.exp(-pre))).astype(BF16)
        hidden[s] = value
        put(s, dot(one_hot, value))
    put(samples, dot(one_hot, jnp.ones((atoms, channels), BF16)))
    for s in range(samples):
        put(samples + 1 + s, dot(one_hot, d_out[s]))


def settle_kernel(own, from_left, from_right, pooled, d_token):
    margin = from_left.shape[1]
    samples = (own.shape[0] - 1) // 2
    middle = own.shape[1]

    def settled(index):
        return jnp.concatenate(
            [own[index, :margin] + from_left[index], own[index, margin:] + from_right[index]], axis=0
        )

    scale = 1.0 / jnp.maximum(settled(samples), 1.0)
    for s in range(samples):
        pooled[s * middle : (s + 1) * middle] = (settled(s) * scale).astype(BF16)
        d_token[s * middle : (s + 1) * middle] = settled(samples + 1 + s).astype(BF16)


def prep_kernel(splits, t_mine, t_other, w_up, w_got, base, extra, w_mix):
    step = pl.program_id(0)
    inner = w_got.shape[2] // 2
    depth = w_got.shape[0] * w_got.shape[1] * 3 // 8
    width = w_up.shape[1]
    channels = w_up.shape[0]
    cut = w_got.shape[1] * 3 // 8
    w_key = w_got[:, :cut, inner:].reshape(depth, inner)
    w_value = w_got[:, cut : 2 * cut, :inner].reshape(depth, inner)
    up = w_up[...].astype(F32)
    up = (up - jnp.mean(up, axis=-1, keepdims=True)).astype(BF16)

    @pl.when(step == 0)
    def _():
        w_mix[:, :inner] = dot(up, w_key).astype(BF16)
        w_mix[:, inner : 2 * inner] = dot(up, w_value).astype(BF16)
        gram = dot_nt(up, up) * (1.0 / width)
        high = gram.astype(BF16)
        w_mix[:, 2 * inner : 2 * inner + channels] = high
        w_mix[:, 2 * inner + channels :] = (gram - high.astype(F32)).astype(BF16)

    def work(t_ref):
        t = t_ref[...].astype(F32)
        cent = (t - jnp.mean(t, axis=-1, keepdims=True)).astype(BF16)
        base[:, :inner] = dot(cent, w_key).astype(BF16)
        base[:, inner:] = dot(cent, w_value).astype(BF16)
        extra[:, :channels] = dot_nt(cent, up) * (2.0 / width)
        wide = cent.astype(F32)
        square = jnp.sum(wide * wide, axis=-1, keepdims=True) * (1.0 / width)
        extra[:, channels:] = jnp.broadcast_to(square, (t.shape[0], channels))

    @pl.when(step < splits)
    def _():
        work(t_mine)

    @pl.when(step >= splits)
    def _():
        work(t_other)


def key_value(tables, bases, extras, w_mix):
    lines, channels = tables[0].shape
    tok, deep = bases[0].shape
    repeat = lines // tok
    y_all = dot(jnp.concatenate(tables, axis=0), w_mix)
    results = []
    for i, (p, base, extra) in enumerate(zip(tables, bases, extras)):
        y = y_all[i * lines : (i + 1) * lines]
        gram = y[:, deep : deep + channels] + y[:, deep + channels :]
        cross = jnp.concatenate([extra[:, :channels]] * repeat, axis=0)
        square = jnp.concatenate([extra[:, channels : channels + 1]] * repeat, axis=0)
        variance = jnp.sum(p.astype(F32) * (gram + cross), axis=-1, keepdims=True) + square
        inverse = lax.rsqrt(jnp.maximum(variance, 0.0) + EPSILON)
        tiled = jnp.concatenate([base.astype(F32)] * repeat, axis=0)
        results.append(((y[:, :deep] + tiled) * inverse).astype(BF16))
    return results


def source(position, core, half):
    own = position < half
    return jnp.where(own, 2 * position + core, 2 * (position - half) + 1 - core)


def half_kernel(
    head_dim,
    place,
    pooled_z,
    base,
    extra,
    w_mix,
    pooled,
    t_own,
    w_up,
    w_got,
    d_token,
    kv,
    tokens_in,
    queries,
    d_normed,
):
    blocks, lines, channels = pooled_z.shape
    samples, _, tok, _ = kv.shape
    inner = w_got.shape[2] // 2
    cut = w_got.shape[1] * 3 // 8
    depth = w_got.shape[0] * cut
    w_query = w_got[:, :cut, :inner].reshape(depth, inner)
    w_down = w_got[:, cut : 2 * cut, inner : inner + channels].reshape(depth, channels)
    t_f = t_own[...].astype(F32)
    for s in range(samples):
        own_rows = slice(s * tok, (s + 1) * tok)
        tokens_in[own_rows] = dot(pooled[own_rows], w_up[...]) + t_f
    normed, _ = normalize(tokens_in[...])
    queries[...] = (dot(normed.astype(BF16), w_query) * (head_dim**-0.5)).astype(BF16)
    d_normed[...] = dot_nt(d_token[...], w_down)

    def step(i, carry):
        which = (2 * i, 2 * i + 1)
        at = [lax.rem(place[0] + source(b, place[2], blocks // 2), blocks) for b in which]
        results = key_value(
            [pooled_z[z] for z in at], [base[b, 0] for b in which], [extra[b, 0] for b in which], w_mix[...]
        )
        for z, result in zip(at, results):
            for s in range(samples):
                kv[s, z] = result[s * tok : (s + 1) * tok]
        return carry

    lax.fori_loop(0, blocks // 2, step, 0)


def attend_kernel(
    heads,
    factor,
    place,
    pooled_y,
    w_mix,
    base_hbm,
    extra_hbm,
    kv_hbm,
    tokens_in,
    queries,
    d_normed,
    w_down,
    w_out,
    bias_hbm,
    proj,
    keep,
    send,
    base,
    extra,
    kv,
    bias,
    scores,
    probs,
    mixed_full,
    inv_sum,
    mixed,
    d_mixed,
    sems,
):
    blocks, lines, channels = pooled_y.shape
    samples, _, _, tok, deep = kv.shape
    total = 2 * blocks * tok
    inner = deep // 2
    head_dim = inner // heads
    half = heads // 2
    rows = half * tok
    span = 256
    starts = (0, inner - span)
    first_z = place[0]
    high = place[1]
    core = place[2]
    pieces_in = min(4, blocks // 2)
    run = blocks // pieces_in

    copies = []
    for piece in range(pieces_in):
        part = pl.ds(piece * run, run)
        copies.append(
            (
                pltpu.make_async_copy(base_hbm.at[part, 1], base.at[part], sems.at[2 * piece]),
                pltpu.make_async_copy(extra_hbm.at[part, 1], extra.at[part], sems.at[2 * piece + 1]),
            )
        )
    bias_copy = pltpu.make_async_copy(bias_hbm, bias, sems.at[2 * pieces_in])
    kv_copies = [
        pltpu.make_async_copy(kv_hbm.at[s], kv.at[s, :, high], sems.at[2 * pieces_in + 1 + s])
        for s in range(samples)
    ]
    for pair in copies:
        for copy in pair:
            copy.start()
    bias_copy.start()
    for copy in kv_copies:
        copy.start()

    for piece in range(pieces_in):
        for copy in copies[piece]:
            copy.wait()

        def step(i, carry):
            which = (2 * i, 2 * i + 1)
            at = [lax.rem(first_z + source(b, core, blocks // 2) + high, blocks) for b in which]
            results = key_value(
                [pooled_y[z] for z in at], [base[b] for b in which], [extra[b] for b in which], w_mix[...]
            )
            for z, result in zip(at, results):
                for s in range(samples):
                    kv[s, z, 1 - high] = result[s * tok : (s + 1) * tok]
            return carry

        lax.fori_loop(piece * run // 2, (piece + 1) * run // 2, step, 0)
    bias_copy.wait()
    for copy in kv_copies:
        copy.wait()

    lane_head = lax.broadcasted_iota(jnp.int32, (rows, span), 1)
    row_head = lax.broadcasted_iota(jnp.int32, (rows, span), 0) // tok

    def head_mask(g):
        lo = (row_head + g * half) * head_dim - starts[g]
        return (lane_head >= lo) & (lane_head < lo + head_dim)

    def spread(values, g):
        tile = values[:, starts[g] : starts[g] + span].astype(F32)
        return jnp.where(head_mask(g), jnp.concatenate([tile] * half, axis=0), 0.0)

    chunk = 512

    def keys(s, start, count, lanes):
        return kv[s, pl.ds(start // (2 * tok), count // (2 * tok)), :, :, lanes].reshape(count, span)

    def forward(s, carry):
        own_rows = pl.ds(pl.multiple_of(s * tok, tok), tok)
        pieces = []
        for g in range(2):
            q = spread(queries[own_rows, :], g).astype(BF16)
            lanes = slice(starts[g], starts[g] + span)
            value_lanes = slice(inner + starts[g], inner + starts[g] + span)
            top = jnp.full((rows, 128), -jnp.inf, F32)
            for j in range(0, total, chunk):
                part = dot_nt(q, keys(s, j, chunk, lanes))
                part = part + bias[g * rows : (g + 1) * rows, j : j + chunk].astype(F32)
                scores[g, :, j : j + chunk] = part
                for c in range(0, chunk, 128):
                    top = jnp.maximum(top, part[:, c : c + 128])
            top = jnp.max(top, axis=-1, keepdims=True)
            amount = jnp.zeros((rows, 128), F32)
            out = jnp.zeros((rows, span), F32)
            for j in range(0, total, chunk):
                e = jnp.exp(scores[g, :, j : j + chunk] - top)
                for c in range(0, chunk, 128):
                    amount = amount + e[:, c : c + 128]
                e = e.astype(BF16)
                probs[s, g, :, j : j + chunk] = e
                out = out + dot(e, keys(s, j, chunk, value_lanes))
            inverse = 1.0 / jnp.sum(amount, axis=-1, keepdims=True)
            out = jnp.where(head_mask(g), out * inverse, 0.0)
            mixed_full[s, g] = out
            inv_sum[s, g] = jnp.broadcast_to(inverse, (rows, 128))
            piece = out[:tok]
            for h in range(1, half):
                piece = piece + out[h * tok : (h + 1) * tok]
            pieces.append(piece)
        cut = starts[1]
        mixed[own_rows, :cut] = pieces[0][:, :cut].astype(BF16)
        mixed[own_rows, cut:span] = (pieces[0][:, cut:] + pieces[1][:, : span - cut]).astype(BF16)
        mixed[own_rows, span:] = pieces[1][:, span - cut :].astype(BF16)
        return carry

    lax.fori_loop(0, samples, forward, 0)

    normed_out, inverse_out = normalize(tokens_in[...] + dot(mixed[...], w_out[...]))
    proj[...] = dot(normed_out.astype(BF16), w_down[...]).astype(BF16)
    d_norm = d_normed[...]
    first = jnp.mean(d_norm, axis=-1, keepdims=True)
    second = jnp.mean(d_norm * normed_out, axis=-1, keepdims=True)
    d_tokens = inverse_out * (d_norm - first - normed_out * second)
    d_mixed[...] = dot_nt(d_tokens.astype(BF16), w_out[...]).astype(BF16)

    for g in range(2):
        value_lanes = slice(inner + starts[g], inner + starts[g] + span)
        wide = []
        delta = []
        scale = []
        for s in range(samples):
            w = spread(d_mixed[s * tok : (s + 1) * tok, :], g)
            wide.append(w.astype(BF16))
            delta.append(jnp.sum(w * mixed_full[s, g], axis=-1, keepdims=True))
            scale.append(inv_sum[s, g][:, :1] * factor)

        def backward(k, carry):
            cols = pl.ds(pl.multiple_of(k * 256, 256), 256)
            grad = None
            for s in range(samples):
                d_prob = dot_nt(wide[s], keys(s, k * 256, 256, value_lanes))
                term = probs[s, g, :, cols].astype(F32) * ((d_prob - delta[s]) * scale[s])
                grad = term if grad is None else grad + term
            low = grad[:, :128]
            high = grad[:, 128:]
            keep[k, g * rows : (g + 1) * rows, :] = jnp.where(core == 0, low, high).astype(BF16)
            send[k, g * rows : (g + 1) * rows, :] = jnp.where(core == 0, high, low).astype(BF16)
            return carry

        lax.fori_loop(0, total // 256, backward, 0)


def decode_kernel(count, token, hidden, proj, from_left, from_right, out):
    samples, atoms, channels = hidden.shape
    tok = proj.shape[1]
    wide = tok + 2 * from_left.shape[1]
    line = lax.broadcasted_iota(jnp.int32, (atoms, wide), 1)
    one_hot = jnp.where(line == token[...], 1.0, 0.0).astype(BF16)
    alive = lax.broadcasted_iota(jnp.int32, (atoms, channels), 0) < count[0]
    for s in range(samples):
        table = jnp.concatenate([from_left[s], proj[s], from_right[s]], axis=0)
        value = hidden[s].astype(F32) + dot(one_hot, table)
        out[s] = jnp.where(alive, value, 0.0).astype(BF16)


def local(
    atom_noised,
    atom_single,
    atom_token,
    atom_count,
    token_single,
    pair_bias,
    w_atom,
    w_up,
    w_query,
    w_key,
    w_value,
    w_out,
    w_down,
    d_atom_out,
):
    samples, atoms, channels = atom_noised.shape
    tok, width = token_single.shape
    margin = tok // 2
    heads, _, total = pair_bias.shape
    n_rows = lax.axis_size("rows")
    n_samp = lax.axis_size("samp")
    inner = w_query.shape[1]
    rank = lax.axis_index("rows")
    group = lax.axis_index("samp")
    chips = n_samp // 2

    sets = [[2 * m + c for m in range(chips)] for c in range(2)]
    swap = [(s, s ^ 1) for s in range(n_samp)]

    spare = jnp.zeros((w_value.shape[0], width - inner - channels), BF16)
    w_own = jnp.concatenate(
        [
            jnp.concatenate([w_query, w_key], axis=1),
            jnp.concatenate([w_value, w_down, spare], axis=1),
            w_out,
            w_up,
        ],
        axis=0,
    )
    w_got = lax.all_gather(w_own, "samp", axis=0, tiled=False)
    cut = w_query.shape[0]
    w_out_all = w_got[:, 2 * cut : 2 * cut + w_out.shape[0]].reshape(-1, width)
    w_up_all = w_got[:, 2 * cut + w_out.shape[0] :].reshape(-1, width)
    w_down_all = w_got[:, cut : 2 * cut, inner : inner + channels].reshape(-1, channels)

    fetched = []
    for part in range(2):
        perm = [
            ((r + 2 * s + part) % n_rows * n_samp + s, r * n_samp + s)
            for r in range(n_rows)
            for s in range(n_samp)
        ]
        fetched.append(lax.ppermute(token_single, ("rows", "samp"), perm))
    fetched = jnp.concatenate(fetched, axis=0)
    t_mine = lax.all_to_all(
        jnp.broadcast_to(fetched[None], (chips,) + fetched.shape), "samp", 0, 0, axis_index_groups=sets, tiled=True
    )
    t_other = lax.ppermute(t_mine, "samp", swap)

    local_token = atom_token - (rank * tok - margin)
    shape = jax.ShapeDtypeStruct
    sums = 2 * samples + 1
    hidden, own, left, right = pl.pallas_call(
        pool_kernel,
        out_shape=(
            shape((samples, atoms, channels), BF16),
            shape((sums, tok, channels), F32),
            shape((sums, margin, channels), F32),
            shape((sums, margin, channels), F32),
        ),
        in_specs=[SCALAR] + [WHOLE] * 5,
        out_specs=(WHOLE,) * 4,
        compiler_params=params(),
        name="pool",
    )(atom_count, local_token[None, :], atom_noised, atom_single, w_atom, d_atom_out)
    up = [(i, i + 1) for i in range(n_rows - 1)]
    down = [(i + 1, i) for i in range(n_rows - 1)]
    from_left = lax.ppermute(right, "rows", up)
    from_right = lax.ppermute(left, "rows", down)
    pooled, d_token = pl.pallas_call(
        settle_kernel,
        out_shape=(shape((samples * tok, channels), BF16), shape((samples * tok, channels), BF16)),
        in_specs=[WHOLE] * 3,
        out_specs=(WHOLE,) * 2,
        compiler_params=params(),
        name="settle",
    )(own, from_left, from_right)
    z_sets = [[2 * z + y for z in range(n_rows // 2)] for y in range(2)]
    pooled_z = lax.all_gather(pooled, "rows", axis=0, tiled=False, axis_index_groups=z_sets)
    pooled_y = lax.ppermute(pooled_z, "rows", [(r, r ^ 1) for r in range(n_rows)])

    block = total // 4
    flat = (chips * 2 * tok, width)
    base, extra, w_mix = pl.pallas_call(
        functools.partial(prep_kernel, 2),
        grid=(4,),
        out_shape=(
            shape((total, 2 * inner), BF16),
            shape((total, 2 * channels), F32),
            shape((channels, 2 * inner + 2 * channels), BF16),
        ),
        in_specs=[
            pl.BlockSpec((block, width), lambda i: (jnp.minimum(i, 1), 0)),
            pl.BlockSpec((block, width), lambda i: (jnp.maximum(i - 2, 0), 0)),
            pl.BlockSpec((channels, width), lambda i: (0, 0)),
            pl.BlockSpec(w_got.shape, lambda i: (0, 0, 0)),
        ],
        out_specs=(
            pl.BlockSpec((block, 2 * inner), lambda i: (i, 0)),
            pl.BlockSpec((block, 2 * channels), lambda i: (i, 0)),
            pl.BlockSpec((channels, 2 * inner + 2 * channels), lambda i: (0, 0)),
        ),
        compiler_params=params(),
        name="prep",
    )(t_mine.reshape(flat), t_other.reshape(flat), w_up_all, w_got)
    blocks = n_rows // 2
    base = base.reshape(blocks, 2, tok, 2 * inner)
    extra = extra.reshape(blocks, 2, tok, 2 * channels)

    place = jnp.stack([rank // 2, rank % 2, group % 2]).astype(jnp.int32)
    kv_half, tokens_in, queries, d_normed = pl.pallas_call(
        functools.partial(half_kernel, inner // heads),
        out_shape=(
            shape((samples, blocks, tok, 2 * inner), BF16),
            shape((samples * tok, width), F32),
            shape((samples * tok, inner), BF16),
            shape((samples * tok, width), F32),
        ),
        in_specs=[SCALAR] + [WHOLE] * 9,
        out_specs=(WHOLE,) * 4,
        compiler_params=params(),
        cost_estimate=pl.CostEstimate(flops=6 * 10**9, bytes_accessed=16 * 10**6, transcendentals=0),
        name="half",
    )(place, pooled_z, base, extra, w_mix, pooled, token_single, w_up_all, w_got, d_token)

    factor = total / (samples * n_samp)
    rows = heads // 2 * tok
    proj, keep, send = pl.pallas_call(
        functools.partial(attend_kernel, heads, factor),
        out_shape=(
            shape((samples * tok, channels), BF16),
            shape((chips, heads * tok, 128), BF16),
            shape((chips, heads * tok, 128), BF16),
        ),
        in_specs=[SCALAR, WHOLE, WHOLE, ANY, ANY, ANY] + [WHOLE] * 5 + [ANY],
        out_specs=(WHOLE,) * 3,
        scratch_shapes=[
            pltpu.VMEM((blocks, tok, 2 * inner), BF16),
            pltpu.VMEM((blocks, tok, 2 * channels), F32),
            pltpu.VMEM((samples, blocks, 2, tok, 2 * inner), BF16),
            pltpu.VMEM((heads * tok, total), BF16),
            pltpu.VMEM((2, rows, total), F32),
            pltpu.VMEM((samples, 2, rows, total), BF16),
            pltpu.VMEM((samples, 2, rows, 256), F32),
            pltpu.VMEM((samples, 2, rows, 128), F32),
            pltpu.VMEM((samples * tok, inner), BF16),
            pltpu.VMEM((samples * tok, inner), BF16),
            pltpu.SemaphoreType.DMA((9 + samples,)),
        ],
        compiler_params=params(),
        name="attend",
    )(
        place,
        pooled_y,
        w_mix,
        base,
        extra,
        kv_half,
        tokens_in,
        queries,
        d_normed,
        w_down_all,
        w_out_all,
        pair_bias.reshape(heads * tok, total),
    )

    other = lax.ppermute(send, "samp", swap)
    both = (keep.astype(F32) + other.astype(F32)).astype(BF16)
    shares = lax.all_to_all(both, "samp", 0, 0, axis_index_groups=sets, tiled=True)
    bias_grad = jnp.sum(shares.astype(F32), axis=0).reshape(heads, tok, 128)

    proj = proj.reshape(samples, tok, channels)
    proj_left = lax.ppermute(proj[:, margin:], "rows", up)
    proj_right = lax.ppermute(proj[:, :margin], "rows", down)
    atom_out = pl.pallas_call(
        decode_kernel,
        out_shape=shape((samples, atoms, channels), BF16),
        in_specs=[SCALAR] + [WHOLE] * 5,
        out_specs=WHOLE,
        compiler_params=params(),
        name="decode",
    )(atom_count, local_token[:, None], hidden, proj, proj_left, proj_right)
    return (atom_out, bias_grad)


def solution(mesh):
    placed = (
        P("samp", "rows", None),
        P("rows", None),
        P("rows"),
        P("rows"),
        P("rows", None),
        P(None, "rows", None),
        P(),
        P("samp", None),
        P("samp", None),
        P("samp", None),
        P("samp", None),
        P("samp", None),
        P("samp", None),
        P("samp", "rows", None),
    )
    return jax.shard_map(
        local,
        mesh=mesh,
        in_specs=placed,
        out_specs=(P("samp", "rows", None), P(None, "rows", "samp")),
        check_vma=False,
    )
```

```python
import functools

import jax
import jax.numpy as jnp
from jax import lax
from jax.experimental import pallas as pl
from jax.experimental.pallas import tpu as pltpu
from jax.sharding import PartitionSpec as P

EPSILON = 1e-05
F32 = jnp.float32
BF16 = jnp.bfloat16
VMEM_BYTES = 56 * 1024 * 1024
WHOLE = pl.BlockSpec(memory_space=pltpu.VMEM)
SCALAR = pl.BlockSpec(memory_space=pltpu.SMEM)
ANY = pl.BlockSpec(memory_space=pl.ANY)


def dot(left, right):
    return lax.dot_general(left, right, (((1,), (0,)), ((), ())), preferred_element_type=F32)


def dot_nt(left, right):
    return lax.dot_general(left, right, (((1,), (1,)), ((), ())), preferred_element_type=F32)


def params():
    return pltpu.CompilerParams(vmem_limit_bytes=VMEM_BYTES)


def normalize(values):
    average = jnp.mean(values, axis=-1, keepdims=True)
    centered = values - average
    variance = jnp.mean(centered * centered, axis=-1, keepdims=True)
    inverse = lax.rsqrt(variance + EPSILON)
    return centered * inverse, inverse


def pool_kernel(count, token, noised, single, w_atom, d_out, hidden, own, left, right):
    samples, atoms, channels = noised.shape
    wide = own.shape[1] + left.shape[1] + right.shape[1]
    margin = left.shape[1]
    middle = own.shape[1]
    slot = lax.broadcasted_iota(jnp.int32, (wide, atoms), 1)
    line = lax.broadcasted_iota(jnp.int32, (wide, atoms), 0)
    picked = (line == token[...]) & (slot < count[0])
    one_hot = jnp.where(picked, 1.0, 0.0).astype(BF16)

    def put(index, sums):
        left[index] = sums[:margin]
        own[index] = sums[margin : margin + middle]
        right[index] = sums[margin + middle :]

    single_f = single[...].astype(F32)
    for s in range(samples):
        query = (noised[s].astype(F32) + single_f).astype(BF16)
        pre = dot(query, w_atom[...])
        value = (query.astype(F32) + pre / (1.0 + jnp.exp(-pre))).astype(BF16)
        hidden[s] = value
        put(s, dot(one_hot, value))
    put(samples, dot(one_hot, jnp.ones((atoms, channels), BF16)))
    for s in range(samples):
        put(samples + 1 + s, dot(one_hot, d_out[s]))


def settle_kernel(own, from_left, from_right, pooled, d_token):
    margin = from_left.shape[1]
    samples = (own.shape[0] - 1) // 2
    middle = own.shape[1]

    def settled(index):
        return jnp.concatenate(
            [own[index, :margin] + from_left[index], own[index, margin:] + from_right[index]], axis=0
        )

    scale = 1.0 / jnp.maximum(settled(samples), 1.0)
    for s in range(samples):
        pooled[s * middle : (s + 1) * middle] = (settled(s) * scale).astype(BF16)
        d_token[s * middle : (s + 1) * middle] = settled(samples + 1 + s).astype(BF16)


def select(rows, cols, size, padded, offset):
    line = lax.broadcasted_iota(jnp.int32, (rows, cols), 0)
    column = lax.broadcasted_iota(jnp.int32, (rows, cols), 1)
    group = line // size
    return jnp.where(column == group * padded + offset + (line - group * size), 1.0, 0.0).astype(BF16)


def pack_kernel(near, far, w_query, w_key, w_value, w_down, w_out, w_up, out):
    tok, width = near.shape
    cut, inner = w_query.shape
    end = inner + w_down.shape[1]
    out[:tok] = near[...]
    out[tok : 2 * tok] = far[...]
    first = slice(2 * tok, 2 * tok + cut)
    second = slice(2 * tok + cut, 2 * tok + 2 * cut)
    out[first, :inner] = w_query[...]
    out[first, inner:] = w_key[...]
    out[second, :inner] = w_value[...]
    out[second, inner:end] = w_down[...]
    out[second, end:] = jnp.zeros((cut, width - end), BF16)
    both = jnp.concatenate([w_out[...].astype(F32), w_up[...].astype(F32)], axis=0)
    out[2 * tok + 2 * cut :] = both.astype(BF16)


def prep_kernel(
    head_dim,
    place,
    got_mine,
    got_other,
    pooled,
    d_token,
    t_own,
    base_hbm,
    extra_hbm,
    w_mix,
    tokens_in,
    queries,
    d_normed,
    weights,
    t_all,
    w_big,
    base,
    extra,
    in_sems,
    out_sems,
):
    chips, height, width = got_mine.shape
    tok = t_own.shape[0]
    block = 2 * tok
    channels = pooled.shape[1]
    samples = pooled.shape[0] // tok
    inner = queries.shape[1]
    core = place[2]
    cut = width // (2 * chips)
    tail = weights.shape[2] - 2 * cut
    up_rows = channels // (2 * chips)
    run = chips // 2

    weight_copies = [
        pltpu.make_async_copy(got_mine.at[:, block:], weights.at[:, core], in_sems.at[0]),
        pltpu.make_async_copy(got_other.at[:, block:], weights.at[:, 1 - core], in_sems.at[1]),
    ]
    t_copies = []
    for i in range(4):
        got = got_mine if i < 2 else got_other
        part = pl.ds((i % 2) * run, run)
        t_copies.append(
            pltpu.make_async_copy(got.at[part, :block], t_all.at[pl.ds(i * run, run)], in_sems.at[2 + i])
        )
    for copy in weight_copies + t_copies:
        copy.start()
    for copy in weight_copies:
        copy.wait()

    rest = weights[:, :, 2 * cut :, :].reshape(2 * chips * tail, width)
    up_raw = dot(select(channels, 2 * chips * tail, up_rows, tail, tail - up_rows), rest)
    up = (up_raw - jnp.mean(up_raw, axis=-1, keepdims=True)).astype(BF16)
    w_big[:, :inner] = weights[:, :, :cut, inner:].reshape(width, inner)
    w_big[:, inner : 2 * inner] = weights[:, :, cut : 2 * cut, :inner].reshape(width, inner)
    w_big[:, 2 * inner :] = up.astype(F32).T.astype(BF16)
    mix = dot(up, w_big[...])
    w_mix[:, : 2 * inner] = mix[:, : 2 * inner].astype(BF16)
    gram = mix[:, 2 * inner :] * (1.0 / width)
    high = gram.astype(BF16)
    w_mix[:, 2 * inner : 2 * inner + channels] = high
    w_mix[:, 2 * inner + channels :] = (gram - high.astype(F32)).astype(BF16)

    outs = []
    for i in range(4):
        t_copies[i].wait()

        def step(k, carry):
            at = i * run + 2 * k
            t = t_all[pl.ds(at, 2)].reshape(2 * block, width).astype(F32)
            cent = (t - jnp.mean(t, axis=-1, keepdims=True)).astype(BF16)
            both = dot(cent, w_big[...])
            base[pl.ds(at, 2)] = both[:, : 2 * inner].astype(BF16).reshape(2, block, 2 * inner)
            wide = cent.astype(F32)
            square = jnp.sum(wide * wide, axis=-1, keepdims=True) * (1.0 / width)
            extra[pl.ds(at, 2), :, :channels] = (both[:, 2 * inner :] * (2.0 / width)).reshape(2, block, channels)
            extra[pl.ds(at, 2), :, channels:] = jnp.broadcast_to(square, (2 * block, channels)).reshape(
                2, block, channels
            )
            return carry

        lax.fori_loop(0, run // 2, step, 0)
        part = pl.ds(i * run, run)
        outs.append(pltpu.make_async_copy(base.at[part], base_hbm.at[part], out_sems.at[2 * i]))
        outs.append(pltpu.make_async_copy(extra.at[part], extra_hbm.at[part], out_sems.at[2 * i + 1]))
        outs[-2].start()
        outs[-1].start()

    w_query = weights[:, :, :cut, :inner].reshape(width, inner)
    w_down = weights[:, :, cut : 2 * cut, inner : inner + channels].reshape(width, channels)
    t_f = t_own[...].astype(F32)
    up_exact = up_raw.astype(BF16)
    for s in range(samples):
        own_rows = slice(s * tok, (s + 1) * tok)
        tokens_in[own_rows] = dot(pooled[own_rows], up_exact) + t_f
    normed, _ = normalize(tokens_in[...])
    queries[...] = (dot(normed.astype(BF16), w_query) * (head_dim**-0.5)).astype(BF16)
    d_normed[...] = dot_nt(d_token[...], w_down)
    for copy in outs:
        copy.wait()


def key_value(tables, bases, extras, w_mix):
    lines, channels = tables[0].shape
    tok, deep = bases[0].shape
    repeat = lines // tok
    y_all = dot(jnp.concatenate(tables, axis=0), w_mix)
    results = []
    for i, (p, base, extra) in enumerate(zip(tables, bases, extras)):
        y = y_all[i * lines : (i + 1) * lines]
        gram = y[:, deep : deep + channels] + y[:, deep + channels :]
        cross = jnp.concatenate([extra[:, :channels]] * repeat, axis=0)
        square = jnp.concatenate([extra[:, channels : channels + 1]] * repeat, axis=0)
        variance = jnp.sum(p.astype(F32) * (gram + cross), axis=-1, keepdims=True) + square
        inverse = lax.rsqrt(jnp.maximum(variance, 0.0) + EPSILON)
        tiled = jnp.concatenate([base.astype(F32)] * repeat, axis=0)
        results.append(((y[:, :deep] + tiled) * inverse).astype(BF16))
    return results


def source(position, core, half):
    own = position < half
    return jnp.where(own, 2 * position + core, 2 * (position - half) + 1 - core)


def attend_kernel(
    heads,
    factor,
    place,
    pooled_z,
    pooled_y,
    w_mix,
    base_hbm,
    extra_hbm,
    tokens_hbm,
    queries,
    d_normed_hbm,
    got_mine,
    got_other,
    bias_hbm,
    proj,
    keep,
    send,
    base,
    extra,
    kv,
    bias,
    tokens_in,
    d_normed,
    w_rest,
    w_down,
    scores,
    probs,
    mixed_full,
    inv_sum,
    mixed,
    d_mixed,
    sems,
):
    blocks, lines, channels = pooled_y.shape
    samples, _, _, tok, deep = kv.shape
    chips, height, width = got_mine.shape
    total = 2 * blocks * tok
    inner = deep // 2
    head_dim = inner // heads
    half = heads // 2
    rows = half * tok
    span = 256
    starts = (0, inner - span)
    first_z = place[0]
    high = place[1]
    core = place[2]
    tail = w_rest.shape[2]
    cut = w_down.shape[2]
    pieces_in = min(4, blocks // 2)
    run = blocks // pieces_in

    def copy(src, dst, index):
        made = pltpu.make_async_copy(src, dst, sems.at[index])
        made.start()
        return made

    copies = []
    for piece in range(pieces_in):
        part = pl.ds(piece * run, run)
        copies.append(
            (
                copy(base_hbm.at[part], base.at[part], 2 * piece),
                copy(extra_hbm.at[part], extra.at[part], 2 * piece + 1),
            )
        )
    down_rows = slice(height - tail - cut, height - tail)
    down_lanes = slice(inner, inner + channels)
    late = [
        copy(bias_hbm, bias, 8),
        copy(tokens_hbm, tokens_in, 9),
        copy(d_normed_hbm, d_normed, 10),
        copy(got_mine.at[:, height - tail :], w_rest.at[:, core], 11),
        copy(got_other.at[:, height - tail :], w_rest.at[:, 1 - core], 12),
        copy(got_mine.at[:, down_rows, down_lanes], w_down.at[:, core], 13),
        copy(got_other.at[:, down_rows, down_lanes], w_down.at[:, 1 - core], 14),
    ]

    for piece in range(pieces_in):
        for made in copies[piece]:
            made.wait()

        def step(b, carry):
            near = lax.rem(first_z + source(b, core, blocks // 2), blocks)
            far = lax.rem(near + high, blocks)
            results = key_value(
                [pooled_z[near], pooled_y[far]],
                [base[b, :tok], base[b, tok:]],
                [extra[b, :tok], extra[b, tok:]],
                w_mix[...],
            )
            for s in range(samples):
                kv[s, near, high] = results[0][s * tok : (s + 1) * tok]
                kv[s, far, 1 - high] = results[1][s * tok : (s + 1) * tok]
            return carry

        lax.fori_loop(piece * run, (piece + 1) * run, step, 0)
    for made in late:
        made.wait()

    lane_head = lax.broadcasted_iota(jnp.int32, (rows, span), 1)
    row_head = lax.broadcasted_iota(jnp.int32, (rows, span), 0) // tok

    def head_mask(g):
        lo = (row_head + g * half) * head_dim - starts[g]
        return (lane_head >= lo) & (lane_head < lo + head_dim)

    def spread(values, g):
        tile = values[:, starts[g] : starts[g] + span].astype(F32)
        return jnp.where(head_mask(g), jnp.concatenate([tile] * half, axis=0), 0.0)

    chunk = 512

    def keys(s, start, count, lanes):
        return kv[s, pl.ds(start // (2 * tok), count // (2 * tok)), :, :, lanes].reshape(count, span)

    def forward(s, carry):
        own_rows = pl.ds(pl.multiple_of(s * tok, tok), tok)
        pieces = []
        for g in range(2):
            q = spread(queries[own_rows, :], g).astype(BF16)
            lanes = slice(starts[g], starts[g] + span)
            value_lanes = slice(inner + starts[g], inner + starts[g] + span)
            top = jnp.full((rows, 128), -jnp.inf, F32)
            for j in range(0, total, chunk):
                part = dot_nt(q, keys(s, j, chunk, lanes))
                part = part + bias[g * rows : (g + 1) * rows, j : j + chunk].astype(F32)
                scores[g, :, j : j + chunk] = part
                for c in range(0, chunk, 128):
                    top = jnp.maximum(top, part[:, c : c + 128])
            top = jnp.max(top, axis=-1, keepdims=True)
            amount = jnp.zeros((rows, 128), F32)
            out = jnp.zeros((rows, span), F32)
            for j in range(0, total, chunk):
                e = jnp.exp(scores[g, :, j : j + chunk] - top)
                for c in range(0, chunk, 128):
                    amount = amount + e[:, c : c + 128]
                e = e.astype(BF16)
                probs[s, g, :, j : j + chunk] = e
                out = out + dot(e, keys(s, j, chunk, value_lanes))
            inverse = 1.0 / jnp.sum(amount, axis=-1, keepdims=True)
            out = jnp.where(head_mask(g), out * inverse, 0.0)
            mixed_full[s, g] = out
            inv_sum[s, g] = jnp.broadcast_to(inverse, (rows, 128))
            piece = out[:tok]
            for h in range(1, half):
                piece = piece + out[h * tok : (h + 1) * tok]
            pieces.append(piece)
        cut = starts[1]
        mixed[own_rows, :cut] = pieces[0][:, :cut].astype(BF16)
        mixed[own_rows, cut:span] = (pieces[0][:, cut:] + pieces[1][:, : span - cut]).astype(BF16)
        mixed[own_rows, span:] = pieces[1][:, span - cut :].astype(BF16)
        return carry

    lax.fori_loop(0, samples, forward, 0)

    rest = w_rest[...].reshape(2 * chips * tail, width)
    down = w_down[...].reshape(width, channels)
    pick = select(inner, 2 * chips * tail, inner // (2 * chips), tail, 0)
    mixed_wide = dot(mixed[...], pick).astype(BF16)
    normed_out, inverse_out = normalize(tokens_in[...] + dot(mixed_wide, rest))
    proj[...] = dot(normed_out.astype(BF16), down).astype(BF16)
    d_norm = d_normed[...]
    first = jnp.mean(d_norm, axis=-1, keepdims=True)
    second = jnp.mean(d_norm * normed_out, axis=-1, keepdims=True)
    d_tokens = inverse_out * (d_norm - first - normed_out * second)
    d_mixed_wide = dot_nt(d_tokens.astype(BF16), rest).astype(BF16)
    d_mixed[...] = dot_nt(d_mixed_wide, pick).astype(BF16)

    for g in range(2):
        value_lanes = slice(inner + starts[g], inner + starts[g] + span)
        wide = []
        delta = []
        scale = []
        for s in range(samples):
            w = spread(d_mixed[s * tok : (s + 1) * tok, :], g)
            wide.append(w.astype(BF16))
            delta.append(jnp.sum(w * mixed_full[s, g], axis=-1, keepdims=True))
            scale.append(inv_sum[s, g][:, :1] * factor)

        def backward(k, carry):
            cols = pl.ds(pl.multiple_of(k * 256, 256), 256)
            grad = None
            for s in range(samples):
                d_prob = dot_nt(wide[s], keys(s, k * 256, 256, value_lanes))
                term = probs[s, g, :, cols].astype(F32) * ((d_prob - delta[s]) * scale[s])
                grad = term if grad is None else grad + term
            low = grad[:, :128]
            high = grad[:, 128:]
            keep[k, g * rows : (g + 1) * rows, :] = jnp.where(core == 0, low, high).astype(BF16)
            send[k, g * rows : (g + 1) * rows, :] = jnp.where(core == 0, high, low).astype(BF16)
            return carry

        lax.fori_loop(0, total // 256, backward, 0)


def decode_kernel(count, token, hidden, proj, from_left, from_right, out):
    samples, atoms, channels = hidden.shape
    tok = proj.shape[1]
    wide = tok + 2 * from_left.shape[1]
    line = lax.broadcasted_iota(jnp.int32, (atoms, wide), 1)
    one_hot = jnp.where(line == token[...], 1.0, 0.0).astype(BF16)
    alive = lax.broadcasted_iota(jnp.int32, (atoms, channels), 0) < count[0]
    for s in range(samples):
        table = jnp.concatenate([from_left[s], proj[s], from_right[s]], axis=0)
        value = hidden[s].astype(F32) + dot(one_hot, table)
        out[s] = jnp.where(alive, value, 0.0).astype(BF16)


def local(
    atom_noised,
    atom_single,
    atom_token,
    atom_count,
    token_single,
    pair_bias,
    w_atom,
    w_up,
    w_query,
    w_key,
    w_value,
    w_out,
    w_down,
    d_atom_out,
):
    samples, atoms, channels = atom_noised.shape
    tok, width = token_single.shape
    margin = tok // 2
    heads, _, total = pair_bias.shape
    n_rows = lax.axis_size("rows")
    n_samp = lax.axis_size("samp")
    inner = w_query.shape[1]
    rank = lax.axis_index("rows")
    group = lax.axis_index("samp")
    chips = n_samp // 2

    blocks = n_rows // 2
    sets = [[2 * m + c for m in range(chips)] for c in range(2)]
    swap = [(s, s ^ 1) for s in range(n_samp)]

    fetched = []
    for part in range(2):
        perm = [
            ((r + 2 * s + part) % n_rows * n_samp + s, r * n_samp + s)
            for r in range(n_rows)
            for s in range(n_samp)
        ]
        fetched.append(lax.ppermute(token_single, ("rows", "samp"), perm))

    local_token = atom_token - (rank * tok - margin)
    shape = jax.ShapeDtypeStruct
    sums = 2 * samples + 1
    hidden, own, left, right = pl.pallas_call(
        pool_kernel,
        out_shape=(
            shape((samples, atoms, channels), BF16),
            shape((sums, tok, channels), F32),
            shape((sums, margin, channels), F32),
            shape((sums, margin, channels), F32),
        ),
        in_specs=[SCALAR] + [WHOLE] * 5,
        out_specs=(WHOLE,) * 4,
        compiler_params=params(),
        name="pool",
    )(atom_count, local_token[None, :], atom_noised, atom_single, w_atom, d_atom_out)
    up = [(i, i + 1) for i in range(n_rows - 1)]
    down = [(i + 1, i) for i in range(n_rows - 1)]


    from_left = lax.ppermute(right, "rows", up)
    from_right = lax.ppermute(left, "rows", down)
    pooled, d_token = pl.pallas_call(
        settle_kernel,
        out_shape=(shape((samples * tok, channels), BF16), shape((samples * tok, channels), BF16)),
        in_specs=[WHOLE] * 3,
        out_specs=(WHOLE,) * 2,
        compiler_params=params(),
        name="settle",
    )(own, from_left, from_right)
    fetched[0], fetched[1], _ = lax.optimization_barrier((fetched[0], fetched[1], left))
    tail = w_out.shape[0] + w_up.shape[0]
    shard = pl.pallas_call(
        pack_kernel,
        out_shape=shape((2 * tok + 2 * w_query.shape[0] + tail, width), BF16),
        in_specs=[WHOLE] * 8,
        out_specs=WHOLE,
        compiler_params=params(),
        name="pack",
    )(fetched[0], fetched[1], w_query, w_key, w_value, w_down, w_out, w_up)
    pooled, shard = lax.optimization_barrier((pooled, shard))
    got_mine = lax.all_gather(shard, "samp", axis=0, tiled=False, axis_index_groups=sets)
    z_sets = [[2 * z + y for z in range(n_rows // 2)] for y in range(2)]
    pooled_z = lax.all_gather(pooled, "rows", axis=0, tiled=False, axis_index_groups=z_sets)
    pooled_y = lax.ppermute(pooled_z, "rows", [(r, r ^ 1) for r in range(n_rows)])

    got_mine, _ = lax.optimization_barrier((got_mine, pooled_z))
    got_other = lax.ppermute(got_mine, "samp", swap)

    place = jnp.stack([rank // 2, rank % 2, group % 2]).astype(jnp.int32)
    weight_rows = shard.shape[0] - 2 * tok
    base, extra, w_mix, tokens_in, queries, d_normed = pl.pallas_call(
        functools.partial(prep_kernel, inner // heads),
        out_shape=(
            shape((blocks, 2 * tok, 2 * inner), BF16),
            shape((blocks, 2 * tok, 2 * channels), F32),
            shape((channels, 2 * inner + 2 * channels), BF16),
            shape((samples * tok, width), F32),
            shape((samples * tok, inner), BF16),
            shape((samples * tok, width), F32),
        ),
        in_specs=[SCALAR, ANY, ANY] + [WHOLE] * 3,
        out_specs=(ANY, ANY) + (WHOLE,) * 4,
        scratch_shapes=[
            pltpu.VMEM((chips, 2, weight_rows, width), BF16),
            pltpu.VMEM((blocks, 2 * tok, width), BF16),
            pltpu.VMEM((width, 2 * inner + channels), BF16),
            pltpu.VMEM((blocks, 2 * tok, 2 * inner), BF16),
            pltpu.VMEM((blocks, 2 * tok, 2 * channels), F32),
            pltpu.SemaphoreType.DMA((6,)),
            pltpu.SemaphoreType.DMA((8,)),
        ],
        compiler_params=params(),
        cost_estimate=pl.CostEstimate(flops=6 * 10**9, bytes_accessed=16 * 10**6, transcendentals=0),
        name="prep",
    )(place, got_mine, got_other, pooled, d_token, token_single)

    factor = total / (samples * n_samp)
    rows = heads // 2 * tok
    proj, keep, send = pl.pallas_call(
        functools.partial(attend_kernel, heads, factor),
        out_shape=(
            shape((samples * tok, channels), BF16),
            shape((chips, heads * tok, 128), BF16),
            shape((chips, heads * tok, 128), BF16),
        ),
        in_specs=[SCALAR, WHOLE, WHOLE, WHOLE, ANY, ANY, ANY, WHOLE, ANY, ANY, ANY, ANY],
        out_specs=(WHOLE,) * 3,
        scratch_shapes=[
            pltpu.VMEM((blocks, 2 * tok, 2 * inner), BF16),
            pltpu.VMEM((blocks, 2 * tok, 2 * channels), F32),
            pltpu.VMEM((samples, blocks, 2, tok, 2 * inner), BF16),
            pltpu.VMEM((heads * tok, total), BF16),
            pltpu.VMEM((samples * tok, width), F32),
            pltpu.VMEM((samples * tok, width), F32),
            pltpu.VMEM((chips, 2, tail, width), BF16),
            pltpu.VMEM((chips, 2, w_down.shape[0], channels), BF16),
            pltpu.VMEM((2, rows, total), F32),
            pltpu.VMEM((samples, 2, rows, total), BF16),
            pltpu.VMEM((samples, 2, rows, 256), F32),
            pltpu.VMEM((samples, 2, rows, 128), F32),
            pltpu.VMEM((samples * tok, inner), BF16),
            pltpu.VMEM((samples * tok, inner), BF16),
            pltpu.SemaphoreType.DMA((15,)),
        ],
        compiler_params=params(),
        name="attend",
    )(
        place,
        pooled_z,
        pooled_y,
        w_mix,
        base,
        extra,
        tokens_in,
        queries,
        d_normed,
        got_mine,
        got_other,
        pair_bias.reshape(heads * tok, total),
    )

    other = lax.ppermute(send, "samp", swap)
    both = (keep.astype(F32) + other.astype(F32)).astype(BF16)
    shares = lax.all_to_all(both, "samp", 0, 0, axis_index_groups=sets, tiled=True)
    bias_grad = jnp.sum(shares.astype(F32), axis=0).reshape(heads, tok, 128)

    proj = proj.reshape(samples, tok, channels)
    proj_left = lax.ppermute(proj[:, margin:], "rows", up)
    proj_right = lax.ppermute(proj[:, :margin], "rows", down)
    atom_out = pl.pallas_call(
        decode_kernel,
        out_shape=shape((samples, atoms, channels), BF16),
        in_specs=[SCALAR] + [WHOLE] * 5,
        out_specs=WHOLE,
        compiler_params=params(),
        name="decode",
    )(atom_count, local_token[:, None], hidden, proj, proj_left, proj_right)
    return (atom_out, bias_grad)


def solution(mesh):
    placed = (
        P("samp", "rows", None),
        P("rows", None),
        P("rows"),
        P("rows"),
        P("rows", None),
        P(None, "rows", None),
        P(),
        P("samp", None),
        P("samp", None),
        P("samp", None),
        P("samp", None),
        P("samp", None),
        P("samp", None),
        P("samp", "rows", None),
    )
    return jax.shard_map(
        local,
        mesh=mesh,
        in_specs=placed,
        out_specs=(P("samp", "rows", None), P(None, "rows", "samp")),
        check_vma=False,
    )
```

```python
import functools

import jax
import jax.numpy as jnp
from jax import lax
from jax.experimental import pallas as pl
from jax.experimental.pallas import tpu as pltpu
from jax.sharding import PartitionSpec as P

EPSILON = 1e-05
F32 = jnp.float32
BF16 = jnp.bfloat16
VMEM_BYTES = 56 * 1024 * 1024
WHOLE = pl.BlockSpec(memory_space=pltpu.VMEM)
SCALAR = pl.BlockSpec(memory_space=pltpu.SMEM)
ANY = pl.BlockSpec(memory_space=pl.ANY)


def dot(left, right):
    return lax.dot_general(left, right, (((1,), (0,)), ((), ())), preferred_element_type=F32)


def dot_nt(left, right):
    return lax.dot_general(left, right, (((1,), (1,)), ((), ())), preferred_element_type=F32)


def params():
    return pltpu.CompilerParams(vmem_limit_bytes=VMEM_BYTES)


def normalize(values):
    average = jnp.mean(values, axis=-1, keepdims=True)
    centered = values - average
    variance = jnp.mean(centered * centered, axis=-1, keepdims=True)
    inverse = lax.rsqrt(variance + EPSILON)
    return centered * inverse, inverse


def pool_kernel(count, token, noised, single, w_atom, d_out, hidden, own, left, right):
    samples, atoms, channels = noised.shape
    wide = own.shape[1] + left.shape[1] + right.shape[1]
    margin = left.shape[1]
    middle = own.shape[1]
    slot = lax.broadcasted_iota(jnp.int32, (wide, atoms), 1)
    line = lax.broadcasted_iota(jnp.int32, (wide, atoms), 0)
    picked = (line == token[...]) & (slot < count[0])
    one_hot = jnp.where(picked, 1.0, 0.0).astype(BF16)

    def put(index, sums):
        left[index] = sums[:margin]
        own[index] = sums[margin : margin + middle]
        right[index] = sums[margin + middle :]

    single_f = single[...].astype(F32)
    for s in range(samples):
        query = (noised[s].astype(F32) + single_f).astype(BF16)
        pre = dot(query, w_atom[...])
        value = (query.astype(F32) + pre / (1.0 + jnp.exp(-pre))).astype(BF16)
        hidden[s] = value
        put(s, dot(one_hot, value))
    put(samples, dot(one_hot, jnp.ones((atoms, channels), BF16)))
    for s in range(samples):
        put(samples + 1 + s, dot(one_hot, d_out[s]))


def settle_kernel(own, from_left, from_right, pooled, d_token):
    margin = from_left.shape[1]
    samples = (own.shape[0] - 1) // 2
    middle = own.shape[1]

    def settled(index):
        return jnp.concatenate(
            [own[index, :margin] + from_left[index], own[index, margin:] + from_right[index]], axis=0
        )

    scale = 1.0 / jnp.maximum(settled(samples), 1.0)
    for s in range(samples):
        pooled[s * middle : (s + 1) * middle] = (settled(s) * scale).astype(BF16)
        d_token[s * middle : (s + 1) * middle] = settled(samples + 1 + s).astype(BF16)


def select(rows, cols, size, padded, offset):
    line = lax.broadcasted_iota(jnp.int32, (rows, cols), 0)
    column = lax.broadcasted_iota(jnp.int32, (rows, cols), 1)
    group = line // size
    return jnp.where(column == group * padded + offset + (line - group * size), 1.0, 0.0).astype(BF16)


def pack_kernel(near, far, w_query, w_key, w_value, w_down, w_out, w_up, out):
    tok, width = near.shape
    cut, inner = w_query.shape
    end = inner + w_down.shape[1]
    out[:tok] = near[...]
    out[tok : 2 * tok] = far[...]
    first = slice(2 * tok, 2 * tok + cut)
    second = slice(2 * tok + cut, 2 * tok + 2 * cut)
    out[first, :inner] = w_query[...]
    out[first, inner:] = w_key[...]
    out[second, :inner] = w_value[...]
    out[second, inner:end] = w_down[...]
    out[second, end:] = jnp.zeros((cut, width - end), BF16)
    both = jnp.concatenate([w_out[...].astype(F32), w_up[...].astype(F32)], axis=0)
    out[2 * tok + 2 * cut :] = both.astype(BF16)


def prep_kernel(
    head_dim,
    got,
    pooled,
    d_token,
    t_own,
    base_hbm,
    extra_hbm,
    w_mix,
    tokens_in,
    queries,
    d_normed,
    weights,
    t_all,
    w_big,
    base,
    extra,
    in_sems,
    out_sems,
):
    members, height, width = got.shape
    tok = t_own.shape[0]
    block = 2 * tok
    channels = pooled.shape[1]
    samples = pooled.shape[0] // tok
    inner = queries.shape[1]
    cut = width // members
    tail = weights.shape[1] - 2 * cut
    up_rows = channels // members
    run = members // 4

    weight_copies = [pltpu.make_async_copy(got.at[:, block:], weights, in_sems.at[0])]
    t_copies = []
    for i in range(4):
        part = pl.ds(i * run, run)
        t_copies.append(pltpu.make_async_copy(got.at[part, :block], t_all.at[part], in_sems.at[1 + i]))
    for copy in weight_copies + t_copies:
        copy.start()
    for copy in weight_copies:
        copy.wait()

    rest = weights[:, 2 * cut :, :].reshape(members * tail, width)
    up_raw = dot(select(channels, members * tail, up_rows, tail, tail - up_rows), rest)
    up = (up_raw - jnp.mean(up_raw, axis=-1, keepdims=True)).astype(BF16)
    w_big[:, :inner] = weights[:, :cut, inner:].reshape(width, inner)
    w_big[:, inner : 2 * inner] = weights[:, cut : 2 * cut, :inner].reshape(width, inner)
    w_big[:, 2 * inner :] = up.astype(F32).T.astype(BF16)
    mix = dot(up, w_big[...])
    w_mix[:, : 2 * inner] = mix[:, : 2 * inner].astype(BF16)
    gram = mix[:, 2 * inner :] * (1.0 / width)
    high = gram.astype(BF16)
    w_mix[:, 2 * inner : 2 * inner + channels] = high
    w_mix[:, 2 * inner + channels :] = (gram - high.astype(F32)).astype(BF16)

    outs = []
    for i in range(4):
        t_copies[i].wait()

        def step(k, carry):
            at = i * run + 2 * k
            t = t_all[pl.ds(at, 2)].reshape(2 * block, width).astype(F32)
            cent = (t - jnp.mean(t, axis=-1, keepdims=True)).astype(BF16)
            both = dot(cent, w_big[...])
            base[pl.ds(at, 2)] = both[:, : 2 * inner].astype(BF16).reshape(2, block, 2 * inner)
            wide = cent.astype(F32)
            square = jnp.sum(wide * wide, axis=-1, keepdims=True) * (1.0 / width)
            extra[pl.ds(at, 2), :, :channels] = (both[:, 2 * inner :] * (2.0 / width)).reshape(2, block, channels)
            extra[pl.ds(at, 2), :, channels:] = jnp.broadcast_to(square, (2 * block, channels)).reshape(
                2, block, channels
            )
            return carry

        lax.fori_loop(0, run // 2, step, 0)
        part = pl.ds(i * run, run)
        outs.append(pltpu.make_async_copy(base.at[part], base_hbm.at[part], out_sems.at[2 * i]))
        outs.append(pltpu.make_async_copy(extra.at[part], extra_hbm.at[part], out_sems.at[2 * i + 1]))
        outs[-2].start()
        outs[-1].start()

    w_query = weights[:, :cut, :inner].reshape(width, inner)
    w_down = weights[:, cut : 2 * cut, inner : inner + channels].reshape(width, channels)
    t_f = t_own[...].astype(F32)
    up_exact = up_raw.astype(BF16)
    for s in range(samples):
        own_rows = slice(s * tok, (s + 1) * tok)
        tokens_in[own_rows] = dot(pooled[own_rows], up_exact) + t_f
    normed, _ = normalize(tokens_in[...])
    queries[...] = (dot(normed.astype(BF16), w_query) * (head_dim**-0.5)).astype(BF16)
    d_normed[...] = dot_nt(d_token[...], w_down)
    for copy in outs:
        copy.wait()


def key_value(tables, bases, extras, w_mix):
    lines, channels = tables[0].shape
    tok, deep = bases[0].shape
    repeat = lines // tok
    y_all = dot(jnp.concatenate(tables, axis=0), w_mix)
    results = []
    for i, (p, base, extra) in enumerate(zip(tables, bases, extras)):
        y = y_all[i * lines : (i + 1) * lines]
        gram = y[:, deep : deep + channels] + y[:, deep + channels :]
        cross = jnp.concatenate([extra[:, :channels]] * repeat, axis=0)
        square = jnp.concatenate([extra[:, channels : channels + 1]] * repeat, axis=0)
        variance = jnp.sum(p.astype(F32) * (gram + cross), axis=-1, keepdims=True) + square
        inverse = lax.rsqrt(jnp.maximum(variance, 0.0) + EPSILON)
        tiled = jnp.concatenate([base.astype(F32)] * repeat, axis=0)
        results.append(((y[:, :deep] + tiled) * inverse).astype(BF16))
    return results


def attend_kernel(
    heads,
    factor,
    place,
    pooled_z,
    pooled_y,
    w_mix,
    base_hbm,
    extra_hbm,
    tokens_hbm,
    queries,
    d_normed_hbm,
    got,
    bias_hbm,
    proj,
    keep,
    send,
    base,
    extra,
    kv,
    bias,
    tokens_in,
    d_normed,
    w_rest,
    w_down,
    scores,
    probs,
    mixed_full,
    inv_sum,
    mixed,
    d_mixed,
    sems,
):
    blocks, lines, channels = pooled_y.shape
    samples, _, _, tok, deep = kv.shape
    members, height, width = got.shape
    total = 2 * blocks * tok
    inner = deep // 2
    head_dim = inner // heads
    half = heads // 2
    rows = half * tok
    span = 256
    starts = (0, inner - span)
    first_z = place[0]
    high = place[1]
    core = place[2]
    tail = w_rest.shape[1]
    cut = w_down.shape[1]
    pieces_in = min(4, blocks // 2)
    run = blocks // pieces_in

    def copy(src, dst, index):
        made = pltpu.make_async_copy(src, dst, sems.at[index])
        made.start()
        return made

    copies = []
    for piece in range(pieces_in):
        part = pl.ds(piece * run, run)
        copies.append(
            (
                copy(base_hbm.at[part], base.at[part], 2 * piece),
                copy(extra_hbm.at[part], extra.at[part], 2 * piece + 1),
            )
        )
    down_rows = slice(height - tail - cut, height - tail)
    down_lanes = slice(inner, inner + channels)
    late = [
        copy(bias_hbm, bias, 8),
        copy(tokens_hbm, tokens_in, 9),
        copy(d_normed_hbm, d_normed, 10),
        copy(got.at[:, height - tail :], w_rest, 11),
        copy(got.at[:, down_rows, down_lanes], w_down, 12),
    ]

    for piece in range(pieces_in):
        for made in copies[piece]:
            made.wait()

        def step(b, carry):
            near = lax.rem(first_z + b, blocks)
            far = lax.rem(near + high, blocks)
            results = key_value(
                [pooled_z[near], pooled_y[far]],
                [base[b, :tok], base[b, tok:]],
                [extra[b, :tok], extra[b, tok:]],
                w_mix[...],
            )
            for s in range(samples):
                kv[s, near, high] = results[0][s * tok : (s + 1) * tok]
                kv[s, far, 1 - high] = results[1][s * tok : (s + 1) * tok]
            return carry

        lax.fori_loop(piece * run, (piece + 1) * run, step, 0)
    for made in late:
        made.wait()

    lane_head = lax.broadcasted_iota(jnp.int32, (rows, span), 1)
    row_head = lax.broadcasted_iota(jnp.int32, (rows, span), 0) // tok

    def head_mask(g):
        lo = (row_head + g * half) * head_dim - starts[g]
        return (lane_head >= lo) & (lane_head < lo + head_dim)

    def spread(values, g):
        tile = values[:, starts[g] : starts[g] + span].astype(F32)
        return jnp.where(head_mask(g), jnp.concatenate([tile] * half, axis=0), 0.0)

    chunk = 512

    def keys(s, start, count, lanes):
        return kv[s, pl.ds(start // (2 * tok), count // (2 * tok)), :, :, lanes].reshape(count, span)

    def forward(s, carry):
        own_rows = pl.ds(pl.multiple_of(s * tok, tok), tok)
        pieces = []
        for g in range(2):
            q = spread(queries[own_rows, :], g).astype(BF16)
            lanes = slice(starts[g], starts[g] + span)
            value_lanes = slice(inner + starts[g], inner + starts[g] + span)
            top = jnp.full((rows, 128), -jnp.inf, F32)
            for j in range(0, total, chunk):
                part = dot_nt(q, keys(s, j, chunk, lanes))
                part = part + bias[g * rows : (g + 1) * rows, j : j + chunk].astype(F32)
                scores[g, :, j : j + chunk] = part
                for c in range(0, chunk, 128):
                    top = jnp.maximum(top, part[:, c : c + 128])
            top = jnp.max(top, axis=-1, keepdims=True)
            amount = jnp.zeros((rows, 128), F32)
            out = jnp.zeros((rows, span), F32)
            for j in range(0, total, chunk):
                e = jnp.exp(scores[g, :, j : j + chunk] - top)
                for c in range(0, chunk, 128):
                    amount = amount + e[:, c : c + 128]
                e = e.astype(BF16)
                probs[s, g, :, j : j + chunk] = e
                out = out + dot(e, keys(s, j, chunk, value_lanes))
            inverse = 1.0 / jnp.sum(amount, axis=-1, keepdims=True)
            out = jnp.where(head_mask(g), out * inverse, 0.0)
            mixed_full[s, g] = out
            inv_sum[s, g] = jnp.broadcast_to(inverse, (rows, 128))
            piece = out[:tok]
            for h in range(1, half):
                piece = piece + out[h * tok : (h + 1) * tok]
            pieces.append(piece)
        cut = starts[1]
        mixed[own_rows, :cut] = pieces[0][:, :cut].astype(BF16)
        mixed[own_rows, cut:span] = (pieces[0][:, cut:] + pieces[1][:, : span - cut]).astype(BF16)
        mixed[own_rows, span:] = pieces[1][:, span - cut :].astype(BF16)
        return carry

    lax.fori_loop(0, samples, forward, 0)

    rest = w_rest[...].reshape(members * tail, width)
    down = w_down[...].reshape(width, channels)
    pick = select(inner, members * tail, inner // members, tail, 0)
    mixed_wide = dot(mixed[...], pick).astype(BF16)
    normed_out, inverse_out = normalize(tokens_in[...] + dot(mixed_wide, rest))
    proj[...] = dot(normed_out.astype(BF16), down).astype(BF16)
    d_norm = d_normed[...]
    first = jnp.mean(d_norm, axis=-1, keepdims=True)
    second = jnp.mean(d_norm * normed_out, axis=-1, keepdims=True)
    d_tokens = inverse_out * (d_norm - first - normed_out * second)
    d_mixed_wide = dot_nt(d_tokens.astype(BF16), rest).astype(BF16)
    d_mixed[...] = dot_nt(d_mixed_wide, pick).astype(BF16)

    for g in range(2):
        value_lanes = slice(inner + starts[g], inner + starts[g] + span)
        wide = []
        delta = []
        scale = []
        for s in range(samples):
            w = spread(d_mixed[s * tok : (s + 1) * tok, :], g)
            wide.append(w.astype(BF16))
            delta.append(jnp.sum(w * mixed_full[s, g], axis=-1, keepdims=True))
            scale.append(inv_sum[s, g][:, :1] * factor)

        def backward(k, carry):
            cols = pl.ds(pl.multiple_of(k * 256, 256), 256)
            grad = None
            for s in range(samples):
                d_prob = dot_nt(wide[s], keys(s, k * 256, 256, value_lanes))
                term = probs[s, g, :, cols].astype(F32) * ((d_prob - delta[s]) * scale[s])
                grad = term if grad is None else grad + term
            low = grad[:, :128]
            high = grad[:, 128:]
            keep[k, g * rows : (g + 1) * rows, :] = jnp.where(core == 0, low, high).astype(BF16)
            send[k, g * rows : (g + 1) * rows, :] = jnp.where(core == 0, high, low).astype(BF16)
            return carry

        lax.fori_loop(0, total // 256, backward, 0)


def decode_kernel(count, token, hidden, proj, from_left, from_right, out):
    samples, atoms, channels = hidden.shape
    tok = proj.shape[1]
    wide = tok + 2 * from_left.shape[1]
    line = lax.broadcasted_iota(jnp.int32, (atoms, wide), 1)
    one_hot = jnp.where(line == token[...], 1.0, 0.0).astype(BF16)
    alive = lax.broadcasted_iota(jnp.int32, (atoms, channels), 0) < count[0]
    for s in range(samples):
        table = jnp.concatenate([from_left[s], proj[s], from_right[s]], axis=0)
        value = hidden[s].astype(F32) + dot(one_hot, table)
        out[s] = jnp.where(alive, value, 0.0).astype(BF16)


def local(
    atom_noised,
    atom_single,
    atom_token,
    atom_count,
    token_single,
    pair_bias,
    w_atom,
    w_up,
    w_query,
    w_key,
    w_value,
    w_out,
    w_down,
    d_atom_out,
):
    samples, atoms, channels = atom_noised.shape
    tok, width = token_single.shape
    margin = tok // 2
    heads, _, total = pair_bias.shape
    n_rows = lax.axis_size("rows")
    n_samp = lax.axis_size("samp")
    inner = w_query.shape[1]
    rank = lax.axis_index("rows")
    group = lax.axis_index("samp")
    chips = n_samp // 2

    blocks = n_rows // 2
    sets = [[2 * m + c for m in range(chips)] for c in range(2)]
    swap = [(s, s ^ 1) for s in range(n_samp)]

    fetched = []
    for part in range(2):
        perm = [
            ((r + 2 * s + part) % n_rows * n_samp + s, r * n_samp + s)
            for r in range(n_rows)
            for s in range(n_samp)
        ]
        fetched.append(lax.ppermute(token_single, ("rows", "samp"), perm))

    local_token = atom_token - (rank * tok - margin)
    shape = jax.ShapeDtypeStruct
    sums = 2 * samples + 1
    hidden, own, left, right = pl.pallas_call(
        pool_kernel,
        out_shape=(
            shape((samples, atoms, channels), BF16),
            shape((sums, tok, channels), F32),
            shape((sums, margin, channels), F32),
            shape((sums, margin, channels), F32),
        ),
        in_specs=[SCALAR] + [WHOLE] * 5,
        out_specs=(WHOLE,) * 4,
        compiler_params=params(),
        name="pool",
    )(atom_count, local_token[None, :], atom_noised, atom_single, w_atom, d_atom_out)
    up = [(i, i + 1) for i in range(n_rows - 1)]
    down = [(i + 1, i) for i in range(n_rows - 1)]

    tail = w_out.shape[0] + w_up.shape[0]
    shard = pl.pallas_call(
        pack_kernel,
        out_shape=shape((2 * tok + 2 * w_query.shape[0] + tail, width), BF16),
        in_specs=[WHOLE] * 8,
        out_specs=WHOLE,
        compiler_params=params(),
        name="pack",
    )(fetched[0], fetched[1], w_query, w_key, w_value, w_down, w_out, w_up)
    got = lax.all_gather(shard, "samp", axis=0, tiled=False)
    left, right, _ = lax.optimization_barrier((left, right, shard))

    from_left = lax.ppermute(right, "rows", up)
    from_right = lax.ppermute(left, "rows", down)
    pooled, d_token = pl.pallas_call(
        settle_kernel,
        out_shape=(shape((samples * tok, channels), BF16), shape((samples * tok, channels), BF16)),
        in_specs=[WHOLE] * 3,
        out_specs=(WHOLE,) * 2,
        compiler_params=params(),
        name="settle",
    )(own, from_left, from_right)
    z_sets = [[2 * z + y for z in range(n_rows // 2)] for y in range(2)]
    pooled_z = lax.all_gather(pooled, "rows", axis=0, tiled=False, axis_index_groups=z_sets)
    pooled_y = lax.ppermute(pooled_z, "rows", [(r, r ^ 1) for r in range(n_rows)])

    got, pooled_y = lax.optimization_barrier((got, pooled_y))

    place = jnp.stack([rank // 2, rank % 2, group % 2]).astype(jnp.int32)
    weight_rows = shard.shape[0] - 2 * tok
    base, extra, w_mix, tokens_in, queries, d_normed = pl.pallas_call(
        functools.partial(prep_kernel, inner // heads),
        out_shape=(
            shape((blocks, 2 * tok, 2 * inner), BF16),
            shape((blocks, 2 * tok, 2 * channels), F32),
            shape((channels, 2 * inner + 2 * channels), BF16),
            shape((samples * tok, width), F32),
            shape((samples * tok, inner), BF16),
            shape((samples * tok, width), F32),
        ),
        in_specs=[ANY] + [WHOLE] * 3,
        out_specs=(ANY, ANY) + (WHOLE,) * 4,
        scratch_shapes=[
            pltpu.VMEM((n_samp, weight_rows, width), BF16),
            pltpu.VMEM((blocks, 2 * tok, width), BF16),
            pltpu.VMEM((width, 2 * inner + channels), BF16),
            pltpu.VMEM((blocks, 2 * tok, 2 * inner), BF16),
            pltpu.VMEM((blocks, 2 * tok, 2 * channels), F32),
            pltpu.SemaphoreType.DMA((5,)),
            pltpu.SemaphoreType.DMA((8,)),
        ],
        compiler_params=params(),
        cost_estimate=pl.CostEstimate(flops=6 * 10**9, bytes_accessed=16 * 10**6, transcendentals=0),
        name="prep",
    )(got, pooled, d_token, token_single)

    factor = total / (samples * n_samp)
    rows = heads // 2 * tok
    proj, keep, send = pl.pallas_call(
        functools.partial(attend_kernel, heads, factor),
        out_shape=(
            shape((samples * tok, channels), BF16),
            shape((chips, heads * tok, 128), BF16),
            shape((chips, heads * tok, 128), BF16),
        ),
        in_specs=[SCALAR, WHOLE, WHOLE, WHOLE, ANY, ANY, ANY, WHOLE, ANY, ANY, ANY],
        out_specs=(WHOLE,) * 3,
        scratch_shapes=[
            pltpu.VMEM((blocks, 2 * tok, 2 * inner), BF16),
            pltpu.VMEM((blocks, 2 * tok, 2 * channels), F32),
            pltpu.VMEM((samples, blocks, 2, tok, 2 * inner), BF16),
            pltpu.VMEM((heads * tok, total), BF16),
            pltpu.VMEM((samples * tok, width), F32),
            pltpu.VMEM((samples * tok, width), F32),
            pltpu.VMEM((n_samp, tail, width), BF16),
            pltpu.VMEM((n_samp, w_down.shape[0], channels), BF16),
            pltpu.VMEM((2, rows, total), F32),
            pltpu.VMEM((samples, 2, rows, total), BF16),
            pltpu.VMEM((samples, 2, rows, 256), F32),
            pltpu.VMEM((samples, 2, rows, 128), F32),
            pltpu.VMEM((samples * tok, inner), BF16),
            pltpu.VMEM((samples * tok, inner), BF16),
            pltpu.SemaphoreType.DMA((13,)),
        ],
        compiler_params=params(),
        name="attend",
    )(
        place,
        pooled_z,
        pooled_y,
        w_mix,
        base,
        extra,
        tokens_in,
        queries,
        d_normed,
        got,
        pair_bias.reshape(heads * tok, total),
    )

    other = lax.ppermute(send, "samp", swap)
    both = (keep.astype(F32) + other.astype(F32)).astype(BF16)
    shares = lax.all_to_all(both, "samp", 0, 0, axis_index_groups=sets, tiled=True)
    bias_grad = jnp.sum(shares.astype(F32), axis=0).reshape(heads, tok, 128)

    proj = proj.reshape(samples, tok, channels)
    proj_left = lax.ppermute(proj[:, margin:], "rows", up)
    proj_right = lax.ppermute(proj[:, :margin], "rows", down)
    atom_out = pl.pallas_call(
        decode_kernel,
        out_shape=shape((samples, atoms, channels), BF16),
        in_specs=[SCALAR] + [WHOLE] * 5,
        out_specs=WHOLE,
        compiler_params=params(),
        name="decode",
    )(atom_count, local_token[:, None], hidden, proj, proj_left, proj_right)
    return (atom_out, bias_grad)


def solution(mesh):
    placed = (
        P("samp", "rows", None),
        P("rows", None),
        P("rows"),
        P("rows"),
        P("rows", None),
        P(None, "rows", None),
        P(),
        P("samp", None),
        P("samp", None),
        P("samp", None),
        P("samp", None),
        P("samp", None),
        P("samp", None),
        P("samp", "rows", None),
    )
    return jax.shard_map(
        local,
        mesh=mesh,
        in_specs=placed,
        out_specs=(P("samp", "rows", None), P(None, "rows", "samp")),
        check_vma=False,
    )
```

```python
import functools

import jax
import jax.numpy as jnp
from jax import lax
from jax.experimental import pallas as pl
from jax.experimental.pallas import tpu as pltpu
from jax.sharding import PartitionSpec as P

EPSILON = 1e-05
F32 = jnp.float32
BF16 = jnp.bfloat16
VMEM_BYTES = 56 * 1024 * 1024
WHOLE = pl.BlockSpec(memory_space=pltpu.VMEM)
SCALAR = pl.BlockSpec(memory_space=pltpu.SMEM)
ANY = pl.BlockSpec(memory_space=pl.ANY)


def dot(left, right):
    return lax.dot_general(left, right, (((1,), (0,)), ((), ())), preferred_element_type=F32)


def dot_nt(left, right):
    return lax.dot_general(left, right, (((1,), (1,)), ((), ())), preferred_element_type=F32)


def params():
    return pltpu.CompilerParams(vmem_limit_bytes=VMEM_BYTES)


def normalize(values):
    average = jnp.mean(values, axis=-1, keepdims=True)
    centered = values - average
    variance = jnp.mean(centered * centered, axis=-1, keepdims=True)
    inverse = lax.rsqrt(variance + EPSILON)
    return centered * inverse, inverse


def pool_kernel(count, token, noised, single, w_atom, d_out, hidden, own, left, right):
    samples, atoms, channels = noised.shape
    wide = own.shape[1] + left.shape[1] + right.shape[1]
    margin = left.shape[1]
    middle = own.shape[1]
    slot = lax.broadcasted_iota(jnp.int32, (wide, atoms), 1)
    line = lax.broadcasted_iota(jnp.int32, (wide, atoms), 0)
    picked = (line == token[...]) & (slot < count[0])
    one_hot = jnp.where(picked, 1.0, 0.0).astype(BF16)

    def put(index, sums):
        left[index] = sums[:margin]
        own[index] = sums[margin : margin + middle]
        right[index] = sums[margin + middle :]

    single_f = single[...].astype(F32)
    for s in range(samples):
        query = (noised[s].astype(F32) + single_f).astype(BF16)
        pre = dot(query, w_atom[...])
        value = (query.astype(F32) + pre / (1.0 + jnp.exp(-pre))).astype(BF16)
        hidden[s] = value
        put(s, dot(one_hot, value))
    put(samples, dot(one_hot, jnp.ones((atoms, channels), BF16)))
    for s in range(samples):
        put(samples + 1 + s, dot(one_hot, d_out[s]))


def settle_kernel(own, from_left, from_right, pooled, d_token):
    margin = from_left.shape[1]
    samples = (own.shape[0] - 1) // 2
    middle = own.shape[1]

    def settled(index):
        return jnp.concatenate(
            [own[index, :margin] + from_left[index], own[index, margin:] + from_right[index]], axis=0
        )

    scale = 1.0 / jnp.maximum(settled(samples), 1.0)
    for s in range(samples):
        pooled[s * middle : (s + 1) * middle] = (settled(s) * scale).astype(BF16)
        d_token[s * middle : (s + 1) * middle] = settled(samples + 1 + s).astype(BF16)


def select(rows, cols, size, padded, offset):
    line = lax.broadcasted_iota(jnp.int32, (rows, cols), 0)
    column = lax.broadcasted_iota(jnp.int32, (rows, cols), 1)
    group = line // size
    return jnp.where(column == group * padded + offset + (line - group * size), 1.0, 0.0).astype(BF16)


def pack_kernel(w_query, w_key, w_value, w_down, w_out, w_up, out):
    cut, inner = w_query.shape
    width = out.shape[1]
    end = inner + w_down.shape[1]
    out[:cut, :inner] = w_query[...]
    out[:cut, inner:] = w_key[...]
    out[cut : 2 * cut, :inner] = w_value[...]
    out[cut : 2 * cut, inner:end] = w_down[...]
    out[cut : 2 * cut, end:] = jnp.zeros((cut, width - end), BF16)
    both = jnp.concatenate([w_out[...].astype(F32), w_up[...].astype(F32)], axis=0)
    out[2 * cut :] = both.astype(BF16)


def prep_kernel(head_dim, weights, pooled, d_token, t_own, w_big, w_mix, tokens_in, queries, d_normed):
    members, height, width = weights.shape
    tok = t_own.shape[0]
    channels = pooled.shape[1]
    samples = pooled.shape[0] // tok
    inner = queries.shape[1]
    cut = width // members
    tail = height - 2 * cut
    up_rows = channels // members

    rest = weights[:, 2 * cut :, :].reshape(members * tail, width)
    up_raw = dot(select(channels, members * tail, up_rows, tail, tail - up_rows), rest)
    up = (up_raw - jnp.mean(up_raw, axis=-1, keepdims=True)).astype(BF16)
    w_big[:, :inner] = weights[:, :cut, inner:].reshape(width, inner)
    w_big[:, inner : 2 * inner] = weights[:, cut : 2 * cut, :inner].reshape(width, inner)
    w_big[:, 2 * inner :] = up.astype(F32).T.astype(BF16)
    mix = dot(up, w_big[...])
    w_mix[:, : 2 * inner] = mix[:, : 2 * inner].astype(BF16)
    gram = mix[:, 2 * inner :] * (1.0 / width)
    high = gram.astype(BF16)
    w_mix[:, 2 * inner : 2 * inner + channels] = high
    w_mix[:, 2 * inner + channels :] = (gram - high.astype(F32)).astype(BF16)

    w_query = weights[:, :cut, :inner].reshape(width, inner)
    w_down = weights[:, cut : 2 * cut, inner : inner + channels].reshape(width, channels)
    t_f = t_own[...].astype(F32)
    up_exact = up_raw.astype(BF16)
    for s in range(samples):
        own_rows = slice(s * tok, (s + 1) * tok)
        tokens_in[own_rows] = dot(pooled[own_rows], up_exact) + t_f
    normed, _ = normalize(tokens_in[...])
    queries[...] = (dot(normed.astype(BF16), w_query) * (head_dim**-0.5)).astype(BF16)
    d_normed[...] = dot_nt(d_token[...], w_down)


def key_value(tables, bases, extras, w_mix):
    lines, channels = tables[0].shape
    tok, deep = bases[0].shape
    repeat = lines // tok
    y_all = dot(jnp.concatenate(tables, axis=0), w_mix)
    results = []
    for i, (p, base, extra) in enumerate(zip(tables, bases, extras)):
        y = y_all[i * lines : (i + 1) * lines]
        gram = y[:, deep : deep + channels] + y[:, deep + channels :]
        cross = jnp.concatenate([extra[:, :channels]] * repeat, axis=0)
        square = jnp.concatenate([extra[:, channels : channels + 1]] * repeat, axis=0)
        variance = jnp.sum(p.astype(F32) * (gram + cross), axis=-1, keepdims=True) + square
        inverse = lax.rsqrt(jnp.maximum(variance, 0.0) + EPSILON)
        tiled = jnp.concatenate([base.astype(F32)] * repeat, axis=0)
        results.append(((y[:, :deep] + tiled) * inverse).astype(BF16))
    return results


def attend_kernel(
    heads,
    factor,
    place,
    pooled_z,
    pooled_y,
    w_mix,
    w_big_hbm,
    got_t,
    tokens_hbm,
    queries,
    d_normed_hbm,
    got,
    bias_hbm,
    proj,
    keep,
    send,
    w_big,
    t_all,
    base,
    extra,
    kv,
    bias,
    tokens_in,
    d_normed,
    w_rest,
    w_down,
    scores,
    probs,
    mixed_full,
    inv_sum,
    mixed,
    d_mixed,
    sems,
):
    blocks, lines, channels = pooled_y.shape
    samples, _, _, tok, deep = kv.shape
    members, height, width = got.shape
    total = 2 * blocks * tok
    inner = deep // 2
    head_dim = inner // heads
    half = heads // 2
    rows = half * tok
    span = 256
    starts = (0, inner - span)
    first_z = place[0]
    high = place[1]
    core = place[2]
    tail = w_rest.shape[1]
    cut = w_down.shape[1]
    pieces_in = min(4, blocks // 2)
    run = blocks // pieces_in

    def copy(src, dst, index):
        made = pltpu.make_async_copy(src, dst, sems.at[index])
        made.start()
        return made

    big_copy = copy(w_big_hbm, w_big, 8)
    copies = []
    for piece in range(pieces_in):
        part = pl.ds(piece * run, run)
        copies.append(copy(got_t.at[part], t_all.at[part], piece))
    down_rows = slice(height - tail - cut, height - tail)
    down_lanes = slice(inner, inner + channels)
    late = [
        copy(bias_hbm, bias, 7),
        copy(tokens_hbm, tokens_in, 9),
        copy(d_normed_hbm, d_normed, 10),
        copy(got.at[:, height - tail :], w_rest, 11),
        copy(got.at[:, down_rows, down_lanes], w_down, 12),
    ]

    big_copy.wait()
    block = 2 * tok
    for piece in range(pieces_in):
        copies[piece].wait()
        part = slice(piece * run, (piece + 1) * run)
        t = t_all[part].reshape(run * block, width).astype(F32)
        cent = (t - jnp.mean(t, axis=-1, keepdims=True)).astype(BF16)
        both = dot(cent, w_big[...])
        base[part] = both[:, :deep].astype(BF16).reshape(run, block, deep)
        wide = cent.astype(F32)
        square = jnp.sum(wide * wide, axis=-1, keepdims=True) * (1.0 / width)
        extra[part, :, :channels] = (both[:, deep:] * (2.0 / width)).reshape(run, block, channels)
        extra[part, :, channels:] = jnp.broadcast_to(square, (run * block, channels)).reshape(run, block, channels)

    def step(b, carry):
        near = lax.rem(first_z + b, blocks)
        far = lax.rem(near + high, blocks)
        results = key_value(
            [pooled_z[near], pooled_y[far]],
            [base[b, :tok], base[b, tok:]],
            [extra[b, :tok], extra[b, tok:]],
            w_mix[...],
        )
        for s in range(samples):
            kv[s, near, high] = results[0][s * tok : (s + 1) * tok]
            kv[s, far, 1 - high] = results[1][s * tok : (s + 1) * tok]
        return carry

    lax.fori_loop(0, blocks, step, 0)
    for made in late:
        made.wait()

    lane_head = lax.broadcasted_iota(jnp.int32, (rows, span), 1)
    row_head = lax.broadcasted_iota(jnp.int32, (rows, span), 0) // tok

    def head_mask(g):
        lo = (row_head + g * half) * head_dim - starts[g]
        return (lane_head >= lo) & (lane_head < lo + head_dim)

    def spread(values, g):
        tile = values[:, starts[g] : starts[g] + span].astype(F32)
        return jnp.where(head_mask(g), jnp.concatenate([tile] * half, axis=0), 0.0)

    chunk = 512

    def keys(s, start, count, lanes):
        return kv[s, pl.ds(start // (2 * tok), count // (2 * tok)), :, :, lanes].reshape(count, span)

    def forward(s, carry):
        own_rows = pl.ds(pl.multiple_of(s * tok, tok), tok)
        pieces = []
        for g in range(2):
            q = spread(queries[own_rows, :], g).astype(BF16)
            lanes = slice(starts[g], starts[g] + span)
            value_lanes = slice(inner + starts[g], inner + starts[g] + span)
            top = jnp.full((rows, 128), -jnp.inf, F32)
            for j in range(0, total, chunk):
                part = dot_nt(q, keys(s, j, chunk, lanes))
                part = part + bias[g * rows : (g + 1) * rows, j : j + chunk].astype(F32)
                scores[g, :, j : j + chunk] = part
                for c in range(0, chunk, 128):
                    top = jnp.maximum(top, part[:, c : c + 128])
            top = jnp.max(top, axis=-1, keepdims=True)
            amount = jnp.zeros((rows, 128), F32)
            out = jnp.zeros((rows, span), F32)
            for j in range(0, total, chunk):
                e = jnp.exp(scores[g, :, j : j + chunk] - top)
                for c in range(0, chunk, 128):
                    amount = amount + e[:, c : c + 128]
                e = e.astype(BF16)
                probs[s, g, :, j : j + chunk] = e
                out = out + dot(e, keys(s, j, chunk, value_lanes))
            inverse = 1.0 / jnp.sum(amount, axis=-1, keepdims=True)
            out = jnp.where(head_mask(g), out * inverse, 0.0)
            mixed_full[s, g] = out
            inv_sum[s, g] = jnp.broadcast_to(inverse, (rows, 128))
            piece = out[:tok]
            for h in range(1, half):
                piece = piece + out[h * tok : (h + 1) * tok]
            pieces.append(piece)
        cut = starts[1]
        mixed[own_rows, :cut] = pieces[0][:, :cut].astype(BF16)
        mixed[own_rows, cut:span] = (pieces[0][:, cut:] + pieces[1][:, : span - cut]).astype(BF16)
        mixed[own_rows, span:] = pieces[1][:, span - cut :].astype(BF16)
        return carry

    lax.fori_loop(0, samples, forward, 0)

    rest = w_rest[...].reshape(members * tail, width)
    down = w_down[...].reshape(width, channels)
    pick = select(inner, members * tail, inner // members, tail, 0)
    mixed_wide = dot(mixed[...], pick).astype(BF16)
    normed_out, inverse_out = normalize(tokens_in[...] + dot(mixed_wide, rest))
    proj[...] = dot(normed_out.astype(BF16), down).astype(BF16)
    d_norm = d_normed[...]
    first = jnp.mean(d_norm, axis=-1, keepdims=True)
    second = jnp.mean(d_norm * normed_out, axis=-1, keepdims=True)
    d_tokens = inverse_out * (d_norm - first - normed_out * second)
    d_mixed_wide = dot_nt(d_tokens.astype(BF16), rest).astype(BF16)
    d_mixed[...] = dot_nt(d_mixed_wide, pick).astype(BF16)

    for g in range(2):
        value_lanes = slice(inner + starts[g], inner + starts[g] + span)
        wide = []
        delta = []
        scale = []
        for s in range(samples):
            w = spread(d_mixed[s * tok : (s + 1) * tok, :], g)
            wide.append(w.astype(BF16))
            delta.append(jnp.sum(w * mixed_full[s, g], axis=-1, keepdims=True))
            scale.append(inv_sum[s, g][:, :1] * factor)

        def backward(k, carry):
            cols = pl.ds(pl.multiple_of(k * 256, 256), 256)
            grad = None
            for s in range(samples):
                d_prob = dot_nt(wide[s], keys(s, k * 256, 256, value_lanes))
                term = probs[s, g, :, cols].astype(F32) * ((d_prob - delta[s]) * scale[s])
                grad = term if grad is None else grad + term
            low = grad[:, :128]
            high = grad[:, 128:]
            keep[k, g * rows : (g + 1) * rows, :] = jnp.where(core == 0, low, high).astype(BF16)
            send[k, g * rows : (g + 1) * rows, :] = jnp.where(core == 0, high, low).astype(BF16)
            return carry

        lax.fori_loop(0, total // 256, backward, 0)


def decode_kernel(count, token, hidden, proj, from_left, from_right, out):
    samples, atoms, channels = hidden.shape
    tok = proj.shape[1]
    wide = tok + 2 * from_left.shape[1]
    line = lax.broadcasted_iota(jnp.int32, (atoms, wide), 1)
    one_hot = jnp.where(line == token[...], 1.0, 0.0).astype(BF16)
    alive = lax.broadcasted_iota(jnp.int32, (atoms, channels), 0) < count[0]
    for s in range(samples):
        table = jnp.concatenate([from_left[s], proj[s], from_right[s]], axis=0)
        value = hidden[s].astype(F32) + dot(one_hot, table)
        out[s] = jnp.where(alive, value, 0.0).astype(BF16)


def local(
    atom_noised,
    atom_single,
    atom_token,
    atom_count,
    token_single,
    pair_bias,
    w_atom,
    w_up,
    w_query,
    w_key,
    w_value,
    w_out,
    w_down,
    d_atom_out,
):
    samples, atoms, channels = atom_noised.shape
    tok, width = token_single.shape
    margin = tok // 2
    heads, _, total = pair_bias.shape
    n_rows = lax.axis_size("rows")
    n_samp = lax.axis_size("samp")
    inner = w_query.shape[1]
    rank = lax.axis_index("rows")
    group = lax.axis_index("samp")
    chips = n_samp // 2

    blocks = n_rows // 2
    sets = [[2 * m + c for m in range(chips)] for c in range(2)]
    swap = [(s, s ^ 1) for s in range(n_samp)]

    shape = jax.ShapeDtypeStruct
    tail = w_out.shape[0] + w_up.shape[0]
    w_own = pl.pallas_call(
        pack_kernel,
        out_shape=shape((2 * w_query.shape[0] + tail, width), BF16),
        in_specs=[WHOLE] * 6,
        out_specs=WHOLE,
        compiler_params=params(),
        name="pack",
    )(w_query, w_key, w_value, w_down, w_out, w_up)
    w_own, atom_noised = lax.optimization_barrier((w_own, atom_noised))
    got = lax.all_gather(w_own, "samp", axis=0, tiled=False)

    fetched = []
    for part in range(2):
        perm = [
            ((r + 2 * s + part) % n_rows * n_samp + s, r * n_samp + s)
            for r in range(n_rows)
            for s in range(n_samp)
        ]
        fetched.append(lax.ppermute(token_single, ("rows", "samp"), perm))

    local_token = atom_token - (rank * tok - margin)
    sums = 2 * samples + 1
    hidden, own, left, right = pl.pallas_call(
        pool_kernel,
        out_shape=(
            shape((samples, atoms, channels), BF16),
            shape((sums, tok, channels), F32),
            shape((sums, margin, channels), F32),
            shape((sums, margin, channels), F32),
        ),
        in_specs=[SCALAR] + [WHOLE] * 5,
        out_specs=(WHOLE,) * 4,
        compiler_params=params(),
        name="pool",
    )(atom_count, local_token[None, :], atom_noised, atom_single, w_atom, d_atom_out)
    up = [(i, i + 1) for i in range(n_rows - 1)]
    down = [(i + 1, i) for i in range(n_rows - 1)]

    from_left = lax.ppermute(right, "rows", up)
    from_right = lax.ppermute(left, "rows", down)
    pooled, d_token = pl.pallas_call(
        settle_kernel,
        out_shape=(shape((samples * tok, channels), BF16), shape((samples * tok, channels), BF16)),
        in_specs=[WHOLE] * 3,
        out_specs=(WHOLE,) * 2,
        compiler_params=params(),
        name="settle",
    )(own, from_left, from_right)
    fetched[0], fetched[1], pooled = lax.optimization_barrier((fetched[0], fetched[1], pooled))
    t_own_pair = jnp.concatenate(fetched, axis=0)
    pooled, t_own_pair = lax.optimization_barrier((pooled, t_own_pair))
    got_t = lax.all_gather(t_own_pair, "samp", axis=0, tiled=False)
    z_sets = [[2 * z + y for z in range(n_rows // 2)] for y in range(2)]
    pooled_z = lax.all_gather(pooled, "rows", axis=0, tiled=False, axis_index_groups=z_sets)
    pooled_y = lax.ppermute(pooled_z, "rows", [(r, r ^ 1) for r in range(n_rows)])

    got_t, pooled_y = lax.optimization_barrier((got_t, pooled_y))

    place = jnp.stack([rank // 2, rank % 2, group % 2]).astype(jnp.int32)
    w_big, w_mix, tokens_in, queries, d_normed = pl.pallas_call(
        functools.partial(prep_kernel, inner // heads),
        out_shape=(
            shape((width, 2 * inner + channels), BF16),
            shape((channels, 2 * inner + 2 * channels), BF16),
            shape((samples * tok, width), F32),
            shape((samples * tok, inner), BF16),
            shape((samples * tok, width), F32),
        ),
        in_specs=[WHOLE] * 4,
        out_specs=(WHOLE,) * 5,
        compiler_params=params(),
        cost_estimate=pl.CostEstimate(flops=2 * 10**9, bytes_accessed=8 * 10**6, transcendentals=0),
        name="prep",
    )(got, pooled, d_token, token_single)

    factor = total / (samples * n_samp)
    rows = heads // 2 * tok
    proj, keep, send = pl.pallas_call(
        functools.partial(attend_kernel, heads, factor),
        out_shape=(
            shape((samples * tok, channels), BF16),
            shape((chips, heads * tok, 128), BF16),
            shape((chips, heads * tok, 128), BF16),
        ),
        in_specs=[SCALAR, WHOLE, WHOLE, WHOLE, ANY, ANY, ANY, WHOLE, ANY, ANY, ANY],
        out_specs=(WHOLE,) * 3,
        scratch_shapes=[
            pltpu.VMEM((width, 2 * inner + channels), BF16),
            pltpu.VMEM((blocks, 2 * tok, width), BF16),
            pltpu.VMEM((blocks, 2 * tok, 2 * inner), BF16),
            pltpu.VMEM((blocks, 2 * tok, 2 * channels), F32),
            pltpu.VMEM((samples, blocks, 2, tok, 2 * inner), BF16),
            pltpu.VMEM((heads * tok, total), BF16),
            pltpu.VMEM((samples * tok, width), F32),
            pltpu.VMEM((samples * tok, width), F32),
            pltpu.VMEM((n_samp, tail, width), BF16),
            pltpu.VMEM((n_samp, w_down.shape[0], channels), BF16),
            pltpu.VMEM((2, rows, total), F32),
            pltpu.VMEM((samples, 2, rows, total), BF16),
            pltpu.VMEM((samples, 2, rows, 256), F32),
            pltpu.VMEM((samples, 2, rows, 128), F32),
            pltpu.VMEM((samples * tok, inner), BF16),
            pltpu.VMEM((samples * tok, inner), BF16),
            pltpu.SemaphoreType.DMA((13,)),
        ],
        compiler_params=params(),
        name="attend",
    )(
        place,
        pooled_z,
        pooled_y,
        w_mix,
        w_big,
        got_t,
        tokens_in,
        queries,
        d_normed,
        got,
        pair_bias.reshape(heads * tok, total),
    )

    other = lax.ppermute(send, "samp", swap)
    both = (keep.astype(F32) + other.astype(F32)).astype(BF16)
    shares = lax.all_to_all(both, "samp", 0, 0, axis_index_groups=sets, tiled=True)
    bias_grad = jnp.sum(shares.astype(F32), axis=0).reshape(heads, tok, 128)

    proj = proj.reshape(samples, tok, channels)
    proj_left = lax.ppermute(proj[:, margin:], "rows", up)
    proj_right = lax.ppermute(proj[:, :margin], "rows", down)
    atom_out = pl.pallas_call(
        decode_kernel,
        out_shape=shape((samples, atoms, channels), BF16),
        in_specs=[SCALAR] + [WHOLE] * 5,
        out_specs=WHOLE,
        compiler_params=params(),
        name="decode",
    )(atom_count, local_token[:, None], hidden, proj, proj_left, proj_right)
    return (atom_out, bias_grad)


def solution(mesh):
    placed = (
        P("samp", "rows", None),
        P("rows", None),
        P("rows"),
        P("rows"),
        P("rows", None),
        P(None, "rows", None),
        P(),
        P("samp", None),
        P("samp", None),
        P("samp", None),
        P("samp", None),
        P("samp", None),
        P("samp", None),
        P("samp", "rows", None),
    )
    return jax.shard_map(
        local,
        mesh=mesh,
        in_specs=placed,
        out_specs=(P("samp", "rows", None), P(None, "rows", "samp")),
        check_vma=False,
    )
```

```python
import functools

import jax
import jax.numpy as jnp
from jax import lax
from jax.experimental import pallas as pl
from jax.experimental.pallas import tpu as pltpu
from jax.sharding import PartitionSpec as P

EPSILON = 1e-05
F32 = jnp.float32
BF16 = jnp.bfloat16
VMEM_BYTES = 56 * 1024 * 1024
WHOLE = pl.BlockSpec(memory_space=pltpu.VMEM)
SCALAR = pl.BlockSpec(memory_space=pltpu.SMEM)
ANY = pl.BlockSpec(memory_space=pl.ANY)


def dot(left, right):
    return lax.dot_general(left, right, (((1,), (0,)), ((), ())), preferred_element_type=F32)


def dot_nt(left, right):
    return lax.dot_general(left, right, (((1,), (1,)), ((), ())), preferred_element_type=F32)


def params():
    return pltpu.CompilerParams(vmem_limit_bytes=VMEM_BYTES)


def normalize(values):
    average = jnp.mean(values, axis=-1, keepdims=True)
    centered = values - average
    variance = jnp.mean(centered * centered, axis=-1, keepdims=True)
    inverse = lax.rsqrt(variance + EPSILON)
    return centered * inverse, inverse


def pool_kernel(count, token, noised, single, w_atom, d_out, hidden, own, left, right):
    samples, atoms, channels = noised.shape
    wide = own.shape[1] + left.shape[1] + right.shape[1]
    margin = left.shape[1]
    middle = own.shape[1]
    slot = lax.broadcasted_iota(jnp.int32, (wide, atoms), 1)
    line = lax.broadcasted_iota(jnp.int32, (wide, atoms), 0)
    picked = (line == token[...]) & (slot < count[0])
    one_hot = jnp.where(picked, 1.0, 0.0).astype(BF16)

    def put(index, sums):
        left[index] = sums[:margin]
        own[index] = sums[margin : margin + middle]
        right[index] = sums[margin + middle :]

    single_f = single[...].astype(F32)
    for s in range(samples):
        query = (noised[s].astype(F32) + single_f).astype(BF16)
        pre = dot(query, w_atom[...])
        value = (query.astype(F32) + pre / (1.0 + jnp.exp(-pre))).astype(BF16)
        hidden[s] = value
        put(s, dot(one_hot, value))
    put(samples, dot(one_hot, jnp.ones((atoms, channels), BF16)))
    for s in range(samples):
        put(samples + 1 + s, dot(one_hot, d_out[s]))


def settle_kernel(own, from_left, from_right, pooled, d_token):
    margin = from_left.shape[1]
    samples = (own.shape[0] - 1) // 2
    middle = own.shape[1]

    def settled(index):
        return jnp.concatenate(
            [own[index, :margin] + from_left[index], own[index, margin:] + from_right[index]], axis=0
        )

    scale = 1.0 / jnp.maximum(settled(samples), 1.0)
    for s in range(samples):
        pooled[s * middle : (s + 1) * middle] = (settled(s) * scale).astype(BF16)
        d_token[s * middle : (s + 1) * middle] = settled(samples + 1 + s).astype(BF16)


def pack_kernel(w_query, w_key, w_value, w_down, w_out, w_up, out):
    cut, inner = w_query.shape
    channels = w_down.shape[1]
    out[:cut, :inner] = w_query[...]
    out[:cut, inner:] = w_key[...]
    value = w_value[...].astype(F32)
    down = w_down[...].astype(F32)
    piece = cut * channels // out.shape[1]
    rest = [
        jnp.concatenate([value[: cut // 2], value[cut // 2 :]], axis=1),
        w_out[...].astype(F32),
        jnp.concatenate([down[i : i + piece] for i in range(0, cut, piece)], axis=1),
        w_up[...].astype(F32),
    ]
    out[cut:] = jnp.concatenate(rest, axis=0).astype(BF16)


def prep_kernel(
    head_dim, got, pooled, d_token, t_own, w_big, w_mix, tokens_in, queries, d_normed, w_out, w_down
):
    members, height, width = got.shape
    tok = t_own.shape[0]
    channels = pooled.shape[1]
    samples = pooled.shape[0] // tok
    inner = queries.shape[1]
    cut = width // members
    half = cut // 2
    out_rows = inner // members
    piece = cut * channels // width

    rest = got[:, cut:, :].astype(F32)
    value = jnp.concatenate([rest[:, :half, :inner], rest[:, :half, inner:]], axis=1).reshape(width, inner)
    at = half + out_rows
    w_out[...] = rest[:, half:at].reshape(inner, width).astype(BF16)
    down = [rest[:, at : at + piece, i : i + channels] for i in range(0, width, channels)]
    w_down[...] = jnp.concatenate(down, axis=1).reshape(width, channels).astype(BF16)
    up_exact = rest[:, at + piece :].reshape(channels, width)
    up = (up_exact - jnp.mean(up_exact, axis=-1, keepdims=True)).astype(BF16)
    w_big[:, :inner] = got[:, :cut, inner:].reshape(width, inner)
    w_big[:, inner : 2 * inner] = value.astype(BF16)
    w_big[:, 2 * inner :] = up.astype(F32).T.astype(BF16)
    mix = dot(up, w_big[...])
    w_mix[:, : 2 * inner] = mix[:, : 2 * inner].astype(BF16)
    gram = mix[:, 2 * inner :] * (1.0 / width)
    high = gram.astype(BF16)
    w_mix[:, 2 * inner : 2 * inner + channels] = high
    w_mix[:, 2 * inner + channels :] = (gram - high.astype(F32)).astype(BF16)

    w_query = got[:, :cut, :inner].reshape(width, inner)
    t_f = t_own[...].astype(F32)
    for s in range(samples):
        own_rows = slice(s * tok, (s + 1) * tok)
        tokens_in[own_rows] = dot(pooled[own_rows], up_exact.astype(BF16)) + t_f
    normed, _ = normalize(tokens_in[...])
    queries[...] = (dot(normed.astype(BF16), w_query) * (head_dim**-0.5)).astype(BF16)
    d_normed[...] = dot_nt(d_token[...], w_down[...])


def attend_kernel(
    heads,
    factor,
    place,
    pooled_z,
    pooled_y,
    w_mix,
    w_big_hbm,
    got_t,
    tokens_hbm,
    queries,
    d_normed_hbm,
    w_out_hbm,
    w_down_hbm,
    bias_hbm,
    proj,
    keep,
    send,
    w_big,
    t_all,
    base,
    extra,
    kv,
    bias,
    tokens_in,
    d_normed,
    w_out,
    w_down,
    scores,
    probs,
    mixed_full,
    inv_sum,
    mixed,
    d_mixed,
    sems,
):
    blocks, lines, channels = pooled_y.shape
    samples, _, _, tok, deep = kv.shape
    width = tokens_in.shape[1]
    total = 2 * blocks * tok
    inner = deep // 2
    head_dim = inner // heads
    half = heads // 2
    rows = half * tok
    span = 256
    starts = (0, inner - span)
    first_z = place[0]
    high = place[1]
    core = place[2]
    pieces_in = min(4, blocks // 2)
    run = blocks // pieces_in

    def copy(src, dst, index):
        made = pltpu.make_async_copy(src, dst, sems.at[index])
        made.start()
        return made

    big_copy = copy(w_big_hbm, w_big, 8)
    copies = []
    for piece in range(pieces_in):
        part = pl.ds(piece * run, run)
        copies.append(copy(got_t.at[part], t_all.at[part], piece))
    late = [
        copy(bias_hbm, bias, 7),
        copy(tokens_hbm, tokens_in, 9),
        copy(d_normed_hbm, d_normed, 10),
        copy(w_out_hbm, w_out, 11),
        copy(w_down_hbm, w_down, 12),
    ]

    big_copy.wait()
    block = 2 * tok
    for piece in range(pieces_in):
        copies[piece].wait()
        part = slice(piece * run, (piece + 1) * run)
        t = t_all[part].reshape(run * block, width).astype(F32)
        cent = (t - jnp.mean(t, axis=-1, keepdims=True)).astype(BF16)
        both = dot(cent, w_big[...])
        base[part] = both[:, :deep].astype(BF16).reshape(run, block, deep)
        wide = cent.astype(F32)
        square = jnp.sum(wide * wide, axis=-1, keepdims=True) * (1.0 / width)
        extra[part, :, :channels] = (both[:, deep:] * (2.0 / width)).reshape(run, block, channels)
        extra[part, :, channels:] = jnp.broadcast_to(square, (run * block, channels)).reshape(run, block, channels)

    def step(b, carry):
        near = lax.rem(first_z + b, blocks)
        far = lax.rem(near + high, blocks)
        p = jnp.concatenate([pooled_z[near], pooled_y[far]], axis=0)
        pf = p.astype(F32)
        gram = dot(p, w_mix[:, deep:])
        inverse = []
        for part in range(2):
            own = slice(part * tok, (part + 1) * tok)
            cross = extra[b, own, :channels]
            square = extra[b, own, channels:]
            for s in range(samples):
                lane = slice(part * lines + s * tok, part * lines + (s + 1) * tok)
                form = pf[lane] * (gram[lane, :channels] + gram[lane, channels:] + cross)
                variance = jnp.sum(form, axis=-1, keepdims=True) + square[:, :1]
                inverse.append(lax.rsqrt(jnp.maximum(variance, 0.0) + EPSILON))
        for c in range(0, deep, span):
            y = dot(p, w_mix[:, c : c + span])
            for part, (z, y_half) in enumerate(((near, high), (far, 1 - high))):
                shared = base[b, part * tok : (part + 1) * tok, c : c + span].astype(F32)
                for s in range(samples):
                    lane = slice(part * lines + s * tok, part * lines + (s + 1) * tok)
                    kv[s, z, y_half, :, c : c + span] = (
                        (y[lane] + shared) * inverse[part * samples + s]
                    ).astype(BF16)
        return carry

    lax.fori_loop(0, blocks, step, 0)
    for made in late:
        made.wait()

    lane_head = lax.broadcasted_iota(jnp.int32, (rows, span), 1)
    row_head = lax.broadcasted_iota(jnp.int32, (rows, span), 0) // tok

    def head_mask(g):
        lo = (row_head + g * half) * head_dim - starts[g]
        return (lane_head >= lo) & (lane_head < lo + head_dim)

    def spread(values, g):
        tile = values[:, starts[g] : starts[g] + span].astype(F32)
        return jnp.where(head_mask(g), jnp.concatenate([tile] * half, axis=0), 0.0)

    chunk = 512

    def keys(s, start, count, lanes):
        return kv[s, pl.ds(start // (2 * tok), count // (2 * tok)), :, :, lanes].reshape(count, span)

    def forward(s, carry):
        own_rows = pl.ds(pl.multiple_of(s * tok, tok), tok)
        pieces = []
        for g in range(2):
            q = spread(queries[own_rows, :], g).astype(BF16)
            lanes = slice(starts[g], starts[g] + span)
            value_lanes = slice(inner + starts[g], inner + starts[g] + span)
            top = jnp.full((rows, 128), -jnp.inf, F32)
            for j in range(0, total, chunk):
                part = dot_nt(q, keys(s, j, chunk, lanes))
                part = part + bias[g * rows : (g + 1) * rows, j : j + chunk].astype(F32)
                scores[g, :, j : j + chunk] = part
                for c in range(0, chunk, 128):
                    top = jnp.maximum(top, part[:, c : c + 128])
            top = jnp.max(top, axis=-1, keepdims=True)
            amount = jnp.zeros((rows, 128), F32)
            out = jnp.zeros((rows, span), F32)
            for j in range(0, total, chunk):
                e = jnp.exp(scores[g, :, j : j + chunk] - top)
                for c in range(0, chunk, 128):
                    amount = amount + e[:, c : c + 128]
                e = e.astype(BF16)
                probs[s, g, :, j : j + chunk] = e
                out = out + dot(e, keys(s, j, chunk, value_lanes))
            inverse = 1.0 / jnp.sum(amount, axis=-1, keepdims=True)
            out = jnp.where(head_mask(g), out * inverse, 0.0)
            mixed_full[s, g] = out
            inv_sum[s, g] = jnp.broadcast_to(inverse, (rows, 128))
            piece = out[:tok]
            for h in range(1, half):
                piece = piece + out[h * tok : (h + 1) * tok]
            pieces.append(piece)
        cut = starts[1]
        mixed[own_rows, :cut] = pieces[0][:, :cut].astype(BF16)
        mixed[own_rows, cut:span] = (pieces[0][:, cut:] + pieces[1][:, : span - cut]).astype(BF16)
        mixed[own_rows, span:] = pieces[1][:, span - cut :].astype(BF16)
        return carry

    lax.fori_loop(0, samples, forward, 0)

    normed_out, inverse_out = normalize(tokens_in[...] + dot(mixed[...], w_out[...]))
    proj[...] = dot(normed_out.astype(BF16), w_down[...]).astype(BF16)
    d_norm = d_normed[...]
    first = jnp.mean(d_norm, axis=-1, keepdims=True)
    second = jnp.mean(d_norm * normed_out, axis=-1, keepdims=True)
    d_tokens = inverse_out * (d_norm - first - normed_out * second)
    d_mixed[...] = dot_nt(d_tokens.astype(BF16), w_out[...]).astype(BF16)

    for g in range(2):
        value_lanes = slice(inner + starts[g], inner + starts[g] + span)
        wide = []
        delta = []
        scale = []
        for s in range(samples):
            w = spread(d_mixed[s * tok : (s + 1) * tok, :], g)
            wide.append(w.astype(BF16))
            delta.append(jnp.sum(w * mixed_full[s, g], axis=-1, keepdims=True))
            scale.append(inv_sum[s, g][:, :1] * factor)

        def backward(k, carry):
            cols = pl.ds(pl.multiple_of(k * 256, 256), 256)
            grad = None
            for s in range(samples):
                d_prob = dot_nt(wide[s], keys(s, k * 256, 256, value_lanes))
                term = probs[s, g, :, cols].astype(F32) * ((d_prob - delta[s]) * scale[s])
                grad = term if grad is None else grad + term
            low = grad[:, :128]
            high = grad[:, 128:]
            keep[k, g * rows : (g + 1) * rows, :] = jnp.where(core == 0, low, high).astype(BF16)
            send[k, g * rows : (g + 1) * rows, :] = jnp.where(core == 0, high, low).astype(BF16)
            return carry

        lax.fori_loop(0, total // 256, backward, 0)


def decode_kernel(count, token, hidden, proj, from_left, from_right, out):
    samples, atoms, channels = hidden.shape
    tok = proj.shape[1]
    wide = tok + 2 * from_left.shape[1]
    line = lax.broadcasted_iota(jnp.int32, (atoms, wide), 1)
    one_hot = jnp.where(line == token[...], 1.0, 0.0).astype(BF16)
    alive = lax.broadcasted_iota(jnp.int32, (atoms, channels), 0) < count[0]
    for s in range(samples):
        table = jnp.concatenate([from_left[s], proj[s], from_right[s]], axis=0)
        value = hidden[s].astype(F32) + dot(one_hot, table)
        out[s] = jnp.where(alive, value, 0.0).astype(BF16)


def local(
    atom_noised,
    atom_single,
    atom_token,
    atom_count,
    token_single,
    pair_bias,
    w_atom,
    w_up,
    w_query,
    w_key,
    w_value,
    w_out,
    w_down,
    d_atom_out,
):
    samples, atoms, channels = atom_noised.shape
    tok, width = token_single.shape
    margin = tok // 2
    heads, _, total = pair_bias.shape
    n_rows = lax.axis_size("rows")
    n_samp = lax.axis_size("samp")
    inner = w_query.shape[1]
    rank = lax.axis_index("rows")
    group = lax.axis_index("samp")
    chips = n_samp // 2

    blocks = n_rows // 2
    sets = [[2 * m + c for m in range(chips)] for c in range(2)]
    swap = [(s, s ^ 1) for s in range(n_samp)]

    shape = jax.ShapeDtypeStruct
    packed = sum(w.size for w in (w_query, w_key, w_value, w_down, w_out, w_up))
    w_own = pl.pallas_call(
        pack_kernel,
        out_shape=shape((packed // width, width), BF16),
        in_specs=[WHOLE] * 6,
        out_specs=WHOLE,
        compiler_params=params(),
        name="pack",
    )(w_query, w_key, w_value, w_down, w_out, w_up)
    w_own, atom_noised = lax.optimization_barrier((w_own, atom_noised))
    got = lax.all_gather(w_own, "samp", axis=0, tiled=False)

    fetched = []
    for part in range(2):
        perm = [
            ((r + 2 * s + part) % n_rows * n_samp + s, r * n_samp + s)
            for r in range(n_rows)
            for s in range(n_samp)
        ]
        fetched.append(lax.ppermute(token_single, ("rows", "samp"), perm))

    local_token = atom_token - (rank * tok - margin)
    sums = 2 * samples + 1
    hidden, own, left, right = pl.pallas_call(
        pool_kernel,
        out_shape=(
            shape((samples, atoms, channels), BF16),
            shape((sums, tok, channels), F32),
            shape((sums, margin, channels), F32),
            shape((sums, margin, channels), F32),
        ),
        in_specs=[SCALAR] + [WHOLE] * 5,
        out_specs=(WHOLE,) * 4,
        compiler_params=params(),
        name="pool",
    )(atom_count, local_token[None, :], atom_noised, atom_single, w_atom, d_atom_out)
    up = [(i, i + 1) for i in range(n_rows - 1)]
    down = [(i + 1, i) for i in range(n_rows - 1)]

    from_left = lax.ppermute(right, "rows", up)
    from_right = lax.ppermute(left, "rows", down)
    pooled, d_token = pl.pallas_call(
        settle_kernel,
        out_shape=(shape((samples * tok, channels), BF16), shape((samples * tok, channels), BF16)),
        in_specs=[WHOLE] * 3,
        out_specs=(WHOLE,) * 2,
        compiler_params=params(),
        name="settle",
    )(own, from_left, from_right)
    fetched[0], fetched[1], pooled = lax.optimization_barrier((fetched[0], fetched[1], pooled))
    t_own_pair = jnp.concatenate(fetched, axis=0)
    pooled, t_own_pair = lax.optimization_barrier((pooled, t_own_pair))
    got_t = lax.all_gather(t_own_pair, "samp", axis=0, tiled=False)
    z_sets = [[2 * z + y for z in range(n_rows // 2)] for y in range(2)]
    pooled_z = lax.all_gather(pooled, "rows", axis=0, tiled=False, axis_index_groups=z_sets)
    pooled_y = lax.ppermute(pooled_z, "rows", [(r, r ^ 1) for r in range(n_rows)])

    got_t, pooled_y = lax.optimization_barrier((got_t, pooled_y))

    place = jnp.stack([rank // 2, rank % 2, group % 2]).astype(jnp.int32)
    w_big, w_mix, tokens_in, queries, d_normed, w_out_all, w_down_all = pl.pallas_call(
        functools.partial(prep_kernel, inner // heads),
        out_shape=(
            shape((width, 2 * inner + channels), BF16),
            shape((channels, 2 * inner + 2 * channels), BF16),
            shape((samples * tok, width), F32),
            shape((samples * tok, inner), BF16),
            shape((samples * tok, width), F32),
            shape((inner, width), BF16),
            shape((width, channels), BF16),
        ),
        in_specs=[WHOLE] * 4,
        out_specs=(WHOLE,) * 7,
        compiler_params=params(),
        cost_estimate=pl.CostEstimate(flops=2 * 10**9, bytes_accessed=8 * 10**6, transcendentals=0),
        name="prep",
    )(got, pooled, d_token, token_single)

    factor = total / (samples * n_samp)
    rows = heads // 2 * tok
    proj, keep, send = pl.pallas_call(
        functools.partial(attend_kernel, heads, factor),
        out_shape=(
            shape((samples * tok, channels), BF16),
            shape((chips, heads * tok, 128), BF16),
            shape((chips, heads * tok, 128), BF16),
        ),
        in_specs=[SCALAR, WHOLE, WHOLE, WHOLE, ANY, ANY, ANY, WHOLE, ANY, ANY, ANY, ANY],
        out_specs=(WHOLE,) * 3,
        scratch_shapes=[
            pltpu.VMEM((width, 2 * inner + channels), BF16),
            pltpu.VMEM((blocks, 2 * tok, width), BF16),
            pltpu.VMEM((blocks, 2 * tok, 2 * inner), BF16),
            pltpu.VMEM((blocks, 2 * tok, 2 * channels), F32),
            pltpu.VMEM((samples, blocks, 2, tok, 2 * inner), BF16),
            pltpu.VMEM((heads * tok, total), BF16),
            pltpu.VMEM((samples * tok, width), F32),
            pltpu.VMEM((samples * tok, width), F32),
            pltpu.VMEM((inner, width), BF16),
            pltpu.VMEM((width, channels), BF16),
            pltpu.VMEM((2, rows, total), F32),
            pltpu.VMEM((samples, 2, rows, total), BF16),
            pltpu.VMEM((samples, 2, rows, 256), F32),
            pltpu.VMEM((samples, 2, rows, 128), F32),
            pltpu.VMEM((samples * tok, inner), BF16),
            pltpu.VMEM((samples * tok, inner), BF16),
            pltpu.SemaphoreType.DMA((13,)),
        ],
        compiler_params=params(),
        name="attend",
    )(
        place,
        pooled_z,
        pooled_y,
        w_mix,
        w_big,
        got_t,
        tokens_in,
        queries,
        d_normed,
        w_out_all,
        w_down_all,
        pair_bias.reshape(heads * tok, total),
    )

    other = lax.ppermute(send, "samp", swap)
    proj = proj.reshape(samples, tok, channels)
    proj_left = lax.ppermute(proj[:, margin:], "rows", up)
    proj_right = lax.ppermute(proj[:, :margin], "rows", down)
    other, proj_left, proj_right = lax.optimization_barrier((other, proj_left, proj_right))
    both = (keep.astype(F32) + other.astype(F32)).astype(BF16)
    shares = lax.all_to_all(both, "samp", 0, 0, axis_index_groups=sets, tiled=True)
    bias_grad = jnp.sum(shares.astype(F32), axis=0).reshape(heads, tok, 128)

    atom_out = pl.pallas_call(
        decode_kernel,
        out_shape=shape((samples, atoms, channels), BF16),
        in_specs=[SCALAR] + [WHOLE] * 5,
        out_specs=WHOLE,
        compiler_params=params(),
        name="decode",
    )(atom_count, local_token[:, None], hidden, proj, proj_left, proj_right)
    return (atom_out, bias_grad)


def solution(mesh):
    placed = (
        P("samp", "rows", None),
        P("rows", None),
        P("rows"),
        P("rows"),
        P("rows", None),
        P(None, "rows", None),
        P(),
        P("samp", None),
        P("samp", None),
        P("samp", None),
        P("samp", None),
        P("samp", None),
        P("samp", None),
        P("samp", "rows", None),
    )
    return jax.shard_map(
        local,
        mesh=mesh,
        in_specs=placed,
        out_specs=(P("samp", "rows", None), P(None, "rows", "samp")),
        check_vma=False,
    )
```

```python
import functools

import jax
import jax.numpy as jnp
from jax import lax
from jax.experimental import pallas as pl
from jax.experimental.pallas import tpu as pltpu
from jax.sharding import PartitionSpec as P

EPSILON = 1e-05
F32 = jnp.float32
BF16 = jnp.bfloat16
VMEM_BYTES = 56 * 1024 * 1024
WHOLE = pl.BlockSpec(memory_space=pltpu.VMEM)
SCALAR = pl.BlockSpec(memory_space=pltpu.SMEM)
ANY = pl.BlockSpec(memory_space=pl.ANY)


def dot(left, right):
    return lax.dot_general(left, right, (((1,), (0,)), ((), ())), preferred_element_type=F32)


def dot_nt(left, right):
    return lax.dot_general(left, right, (((1,), (1,)), ((), ())), preferred_element_type=F32)


def params():
    return pltpu.CompilerParams(vmem_limit_bytes=VMEM_BYTES)


def normalize(values):
    average = jnp.mean(values, axis=-1, keepdims=True)
    centered = values - average
    variance = jnp.mean(centered * centered, axis=-1, keepdims=True)
    inverse = lax.rsqrt(variance + EPSILON)
    return centered * inverse, inverse


def pool_kernel(count, token, noised, single, w_atom, d_out, hidden, own, left, right):
    samples, atoms, channels = noised.shape
    wide = own.shape[1] + left.shape[1] + right.shape[1]
    margin = left.shape[1]
    middle = own.shape[1]
    slot = lax.broadcasted_iota(jnp.int32, (wide, atoms), 1)
    line = lax.broadcasted_iota(jnp.int32, (wide, atoms), 0)
    picked = (line == token[...]) & (slot < count[0])
    one_hot = jnp.where(picked, 1.0, 0.0).astype(BF16)

    def put(index, sums):
        left[index] = sums[:margin]
        own[index] = sums[margin : margin + middle]
        right[index] = sums[margin + middle :]

    single_f = single[...].astype(F32)
    for s in range(samples):
        query = (noised[s].astype(F32) + single_f).astype(BF16)
        pre = dot(query, w_atom[...])
        value = (query.astype(F32) + pre / (1.0 + jnp.exp(-pre))).astype(BF16)
        hidden[s] = value
        put(s, dot(one_hot, value))
    put(samples, dot(one_hot, jnp.ones((atoms, channels), BF16)))
    for s in range(samples):
        put(samples + 1 + s, dot(one_hot, d_out[s]))


def settle_kernel(own, from_left, from_right, pooled, d_token):
    margin = from_left.shape[1]
    samples = (own.shape[0] - 1) // 2
    middle = own.shape[1]

    def settled(index):
        return jnp.concatenate(
            [own[index, :margin] + from_left[index], own[index, margin:] + from_right[index]], axis=0
        )

    scale = 1.0 / jnp.maximum(settled(samples), 1.0)
    for s in range(samples):
        pooled[s * middle : (s + 1) * middle] = (settled(s) * scale).astype(BF16)
        d_token[s * middle : (s + 1) * middle] = settled(samples + 1 + s).astype(BF16)


def pack_kernel(w_query, w_key, w_value, w_down, w_out, w_up, out):
    cut, inner = w_query.shape
    channels = w_down.shape[1]
    out[:cut, :inner] = w_query[...]
    out[:cut, inner:] = w_key[...]
    value = w_value[...].astype(F32)
    down = w_down[...].astype(F32)
    piece = cut * channels // out.shape[1]
    rest = [
        jnp.concatenate([value[: cut // 2], value[cut // 2 :]], axis=1),
        w_out[...].astype(F32),
        jnp.concatenate([down[i : i + piece] for i in range(0, cut, piece)], axis=1),
        w_up[...].astype(F32),
    ]
    out[cut:] = jnp.concatenate(rest, axis=0).astype(BF16)


def prep_kernel(
    head_dim, got, pooled, d_token, t_own, w_big, w_mix, tokens_in, queries, d_normed, w_out, w_down
):
    members, height, width = got.shape
    tok = t_own.shape[0]
    channels = pooled.shape[1]
    samples = pooled.shape[0] // tok
    inner = queries.shape[1]
    cut = width // members
    half = cut // 2
    out_rows = inner // members
    piece = cut * channels // width

    rest = got[:, cut:, :].astype(F32)
    value = jnp.concatenate([rest[:, :half, :inner], rest[:, :half, inner:]], axis=1).reshape(width, inner)
    at = half + out_rows
    w_out[...] = rest[:, half:at].reshape(inner, width).astype(BF16)
    down = [rest[:, at : at + piece, i : i + channels] for i in range(0, width, channels)]
    w_down[...] = jnp.concatenate(down, axis=1).reshape(width, channels).astype(BF16)
    up_exact = rest[:, at + piece :].reshape(channels, width)
    up = (up_exact - jnp.mean(up_exact, axis=-1, keepdims=True)).astype(BF16)
    w_big[:, :inner] = got[:, :cut, inner:].reshape(width, inner)
    w_big[:, inner : 2 * inner] = value.astype(BF16)
    w_big[:, 2 * inner :] = up.astype(F32).T.astype(BF16)
    mix = dot(up, w_big[...])
    w_mix[:, : 2 * inner] = mix[:, : 2 * inner].astype(BF16)
    gram = mix[:, 2 * inner :] * (1.0 / width)
    high = gram.astype(BF16)
    w_mix[:, 2 * inner : 2 * inner + channels] = high
    w_mix[:, 2 * inner + channels :] = (gram - high.astype(F32)).astype(BF16)

    w_query = got[:, :cut, :inner].reshape(width, inner)
    t_f = t_own[...].astype(F32)
    for s in range(samples):
        own_rows = slice(s * tok, (s + 1) * tok)
        tokens_in[own_rows] = dot(pooled[own_rows], up_exact.astype(BF16)) + t_f
    normed, _ = normalize(tokens_in[...])
    queries[...] = (dot(normed.astype(BF16), w_query) * (head_dim**-0.5)).astype(BF16)
    d_normed[...] = dot_nt(d_token[...], w_down[...])


def attend_kernel(
    heads,
    factor,
    place,
    pooled_z,
    pooled_y,
    w_mix,
    w_big_hbm,
    got_t,
    tokens_hbm,
    queries,
    d_normed_hbm,
    w_out_hbm,
    w_down_hbm,
    bias_hbm,
    proj,
    keep,
    send,
    w_big,
    t_all,
    base,
    extra,
    kv,
    bias,
    tokens_in,
    d_normed,
    w_out,
    w_down,
    scores,
    probs,
    mixed_full,
    inv_sum,
    mixed,
    d_mixed,
    sems,
):
    blocks, lines, channels = pooled_y.shape
    samples, _, _, tok, deep = kv.shape
    width = tokens_in.shape[1]
    total = 2 * blocks * tok
    inner = deep // 2
    head_dim = inner // heads
    half = heads // 2
    rows = half * tok
    span = 256
    starts = (0, inner - span)
    first_z = place[0]
    high = place[1]
    core = place[2]
    pieces_in = min(4, blocks // 2)
    run = blocks // pieces_in

    def copy(src, dst, index):
        made = pltpu.make_async_copy(src, dst, sems.at[index])
        made.start()
        return made

    big_copy = copy(w_big_hbm, w_big, 8)
    copies = []
    for piece in range(pieces_in):
        part = pl.ds(piece * run, run)
        copies.append(copy(got_t.at[part], t_all.at[part], piece))
    late = [
        copy(bias_hbm, bias, 7),
        copy(tokens_hbm, tokens_in, 9),
        copy(d_normed_hbm, d_normed, 10),
        copy(w_out_hbm, w_out, 11),
        copy(w_down_hbm, w_down, 12),
    ]

    big_copy.wait()
    block = 2 * tok
    for piece in range(pieces_in):
        copies[piece].wait()
        part = slice(piece * run, (piece + 1) * run)
        t = t_all[part].reshape(run * block, width).astype(F32)
        cent = (t - jnp.mean(t, axis=-1, keepdims=True)).astype(BF16)
        both = dot(cent, w_big[...])
        base[part] = both[:, :deep].astype(BF16).reshape(run, block, deep)
        wide = cent.astype(F32)
        square = jnp.sum(wide * wide, axis=-1, keepdims=True) * (1.0 / width)
        extra[part, :, :channels] = (both[:, deep:] * (2.0 / width)).reshape(run, block, channels)
        extra[part, :, channels:] = jnp.broadcast_to(square, (run * block, channels)).reshape(run, block, channels)

    def step(b, carry):
        near = lax.rem(first_z + b, blocks)
        far = lax.rem(near + high, blocks)
        p = jnp.concatenate([pooled_z[near], pooled_y[far]], axis=0)
        pf = p.astype(F32)
        gram = dot(p, w_mix[:, deep:])
        inverse = []
        for part in range(2):
            own = slice(part * tok, (part + 1) * tok)
            cross = extra[b, own, :channels]
            square = extra[b, own, channels:]
            for s in range(samples):
                lane = slice(part * lines + s * tok, part * lines + (s + 1) * tok)
                form = pf[lane] * (gram[lane, :channels] + gram[lane, channels:] + cross)
                variance = jnp.sum(form, axis=-1, keepdims=True) + square[:, :1]
                inverse.append(lax.rsqrt(jnp.maximum(variance, 0.0) + EPSILON))
        for c in range(0, deep, span):
            y = dot(p, w_mix[:, c : c + span])
            for part, (z, y_half) in enumerate(((near, high), (far, 1 - high))):
                shared = base[b, part * tok : (part + 1) * tok, c : c + span].astype(F32)
                for s in range(samples):
                    lane = slice(part * lines + s * tok, part * lines + (s + 1) * tok)
                    kv[s, z, y_half, :, c : c + span] = (
                        (y[lane] + shared) * inverse[part * samples + s]
                    ).astype(BF16)
        return carry

    lax.fori_loop(0, blocks, step, 0)
    for made in late:
        made.wait()

    lane_head = lax.broadcasted_iota(jnp.int32, (rows, span), 1)
    row_head = lax.broadcasted_iota(jnp.int32, (rows, span), 0) // tok

    def head_mask(g):
        lo = (row_head + g * half) * head_dim - starts[g]
        return (lane_head >= lo) & (lane_head < lo + head_dim)

    def spread(values, g):
        tile = values[:, starts[g] : starts[g] + span].astype(F32)
        return jnp.where(head_mask(g), jnp.concatenate([tile] * half, axis=0), 0.0)

    chunk = 512

    def keys(s, start, count, lanes):
        return kv[s, pl.ds(start // (2 * tok), count // (2 * tok)), :, :, lanes].reshape(count, span)

    def forward(s, carry):
        own_rows = pl.ds(pl.multiple_of(s * tok, tok), tok)
        pieces = []
        for g in range(2):
            q = spread(queries[own_rows, :], g).astype(BF16)
            lanes = slice(starts[g], starts[g] + span)
            value_lanes = slice(inner + starts[g], inner + starts[g] + span)
            top = jnp.full((rows, 128), -jnp.inf, F32)
            for j in range(0, total, span):
                part = dot_nt(q, keys(s, j, span, lanes))
                part = part + bias[g * rows : (g + 1) * rows, j : j + span].astype(F32)
                scores[g, :, j : j + span] = part
                for c in range(0, span, 128):
                    top = jnp.maximum(top, part[:, c : c + 128])
            top = jnp.max(top, axis=-1, keepdims=True)
            amount = jnp.zeros((rows, 128), F32)
            out = jnp.zeros((rows, span), F32)
            for j in range(0, total, chunk):
                e = jnp.exp(scores[g, :, j : j + chunk] - top)
                for c in range(0, chunk, 128):
                    amount = amount + e[:, c : c + 128]
                e = e.astype(BF16)
                probs[s, g, :, j : j + chunk] = e
                out = out + dot(e, keys(s, j, chunk, value_lanes))
            inverse = 1.0 / jnp.sum(amount, axis=-1, keepdims=True)
            out = jnp.where(head_mask(g), out * inverse, 0.0)
            mixed_full[s, g] = out
            inv_sum[s, g] = jnp.broadcast_to(inverse, (rows, 128))
            piece = out[:tok]
            for h in range(1, half):
                piece = piece + out[h * tok : (h + 1) * tok]
            pieces.append(piece)
        cut = starts[1]
        mixed[own_rows, :cut] = pieces[0][:, :cut].astype(BF16)
        mixed[own_rows, cut:span] = (pieces[0][:, cut:] + pieces[1][:, : span - cut]).astype(BF16)
        mixed[own_rows, span:] = pieces[1][:, span - cut :].astype(BF16)
        return carry

    lax.fori_loop(0, samples, forward, 0)

    normed_out, inverse_out = normalize(tokens_in[...] + dot(mixed[...], w_out[...]))
    proj[...] = dot(normed_out.astype(BF16), w_down[...]).astype(BF16)
    d_norm = d_normed[...]
    first = jnp.mean(d_norm, axis=-1, keepdims=True)
    second = jnp.mean(d_norm * normed_out, axis=-1, keepdims=True)
    d_tokens = inverse_out * (d_norm - first - normed_out * second)
    d_mixed[...] = dot_nt(d_tokens.astype(BF16), w_out[...]).astype(BF16)

    for g in range(2):
        value_lanes = slice(inner + starts[g], inner + starts[g] + span)
        wide = []
        delta = []
        scale = []
        for s in range(samples):
            w = spread(d_mixed[s * tok : (s + 1) * tok, :], g)
            wide.append(w.astype(BF16))
            delta.append(jnp.sum(w * mixed_full[s, g], axis=-1, keepdims=True))
            scale.append(inv_sum[s, g][:, :1] * factor)

        def backward(k, carry):
            cols = pl.ds(pl.multiple_of(k * 256, 256), 256)
            grad = None
            for s in range(samples):
                d_prob = dot_nt(wide[s], keys(s, k * 256, 256, value_lanes))
                term = probs[s, g, :, cols].astype(F32) * ((d_prob - delta[s]) * scale[s])
                grad = term if grad is None else grad + term
            low = grad[:, :128]
            high = grad[:, 128:]
            keep[k, g * rows : (g + 1) * rows, :] = jnp.where(core == 0, low, high).astype(BF16)
            send[k, g * rows : (g + 1) * rows, :] = jnp.where(core == 0, high, low).astype(BF16)
            return carry

        lax.fori_loop(0, total // 256, backward, 0)


def decode_kernel(count, token, hidden, proj, from_left, from_right, out):
    samples, atoms, channels = hidden.shape
    tok = proj.shape[1]
    wide = tok + 2 * from_left.shape[1]
    line = lax.broadcasted_iota(jnp.int32, (atoms, wide), 1)
    one_hot = jnp.where(line == token[...], 1.0, 0.0).astype(BF16)
    alive = lax.broadcasted_iota(jnp.int32, (atoms, channels), 0) < count[0]
    for s in range(samples):
        table = jnp.concatenate([from_left[s], proj[s], from_right[s]], axis=0)
        value = hidden[s].astype(F32) + dot(one_hot, table)
        out[s] = jnp.where(alive, value, 0.0).astype(BF16)


def local(
    atom_noised,
    atom_single,
    atom_token,
    atom_count,
    token_single,
    pair_bias,
    w_atom,
    w_up,
    w_query,
    w_key,
    w_value,
    w_out,
    w_down,
    d_atom_out,
):
    samples, atoms, channels = atom_noised.shape
    tok, width = token_single.shape
    margin = tok // 2
    heads, _, total = pair_bias.shape
    n_rows = lax.axis_size("rows")
    n_samp = lax.axis_size("samp")
    inner = w_query.shape[1]
    rank = lax.axis_index("rows")
    group = lax.axis_index("samp")
    chips = n_samp // 2

    blocks = n_rows // 2
    sets = [[2 * m + c for m in range(chips)] for c in range(2)]
    swap = [(s, s ^ 1) for s in range(n_samp)]

    shape = jax.ShapeDtypeStruct
    packed = sum(w.size for w in (w_query, w_key, w_value, w_down, w_out, w_up))
    w_own = pl.pallas_call(
        pack_kernel,
        out_shape=shape((packed // width, width), BF16),
        in_specs=[WHOLE] * 6,
        out_specs=WHOLE,
        compiler_params=params(),
        name="pack",
    )(w_query, w_key, w_value, w_down, w_out, w_up)
    w_own, atom_noised = lax.optimization_barrier((w_own, atom_noised))
    got = lax.all_gather(w_own, "samp", axis=0, tiled=False)

    fetched = []
    for part in range(2):
        perm = [
            ((r + 2 * s + part) % n_rows * n_samp + s, r * n_samp + s)
            for r in range(n_rows)
            for s in range(n_samp)
        ]
        fetched.append(lax.ppermute(token_single, ("rows", "samp"), perm))

    local_token = atom_token - (rank * tok - margin)
    sums = 2 * samples + 1
    hidden, own, left, right = pl.pallas_call(
        pool_kernel,
        out_shape=(
            shape((samples, atoms, channels), BF16),
            shape((sums, tok, channels), F32),
            shape((sums, margin, channels), F32),
            shape((sums, margin, channels), F32),
        ),
        in_specs=[SCALAR] + [WHOLE] * 5,
        out_specs=(WHOLE,) * 4,
        compiler_params=params(),
        name="pool",
    )(atom_count, local_token[None, :], atom_noised, atom_single, w_atom, d_atom_out)
    up = [(i, i + 1) for i in range(n_rows - 1)]
    down = [(i + 1, i) for i in range(n_rows - 1)]

    from_left = lax.ppermute(right, "rows", up)
    from_right = lax.ppermute(left, "rows", down)
    pooled, d_token = pl.pallas_call(
        settle_kernel,
        out_shape=(shape((samples * tok, channels), BF16), shape((samples * tok, channels), BF16)),
        in_specs=[WHOLE] * 3,
        out_specs=(WHOLE,) * 2,
        compiler_params=params(),
        name="settle",
    )(own, from_left, from_right)
    fetched[0], fetched[1], pooled = lax.optimization_barrier((fetched[0], fetched[1], pooled))
    t_own_pair = jnp.concatenate(fetched, axis=0)
    pooled, t_own_pair = lax.optimization_barrier((pooled, t_own_pair))
    got_t = lax.all_gather(t_own_pair, "samp", axis=0, tiled=False)
    z_sets = [[2 * z + y for z in range(n_rows // 2)] for y in range(2)]
    pooled_z = lax.all_gather(pooled, "rows", axis=0, tiled=False, axis_index_groups=z_sets)
    pooled_y = lax.ppermute(pooled_z, "rows", [(r, r ^ 1) for r in range(n_rows)])

    got_t, pooled_y = lax.optimization_barrier((got_t, pooled_y))

    place = jnp.stack([rank // 2, rank % 2, group % 2]).astype(jnp.int32)
    w_big, w_mix, tokens_in, queries, d_normed, w_out_all, w_down_all = pl.pallas_call(
        functools.partial(prep_kernel, inner // heads),
        out_shape=(
            shape((width, 2 * inner + channels), BF16),
            shape((channels, 2 * inner + 2 * channels), BF16),
            shape((samples * tok, width), F32),
            shape((samples * tok, inner), BF16),
            shape((samples * tok, width), F32),
            shape((inner, width), BF16),
            shape((width, channels), BF16),
        ),
        in_specs=[WHOLE] * 4,
        out_specs=(WHOLE,) * 7,
        compiler_params=params(),
        cost_estimate=pl.CostEstimate(flops=2 * 10**9, bytes_accessed=8 * 10**6, transcendentals=0),
        name="prep",
    )(got, pooled, d_token, token_single)

    factor = total / (samples * n_samp)
    rows = heads // 2 * tok
    proj, keep, send = pl.pallas_call(
        functools.partial(attend_kernel, heads, factor),
        out_shape=(
            shape((samples * tok, channels), BF16),
            shape((chips, heads * tok, 128), BF16),
            shape((chips, heads * tok, 128), BF16),
        ),
        in_specs=[SCALAR, WHOLE, WHOLE, WHOLE, ANY, ANY, ANY, WHOLE, ANY, ANY, ANY, ANY],
        out_specs=(WHOLE,) * 3,
        scratch_shapes=[
            pltpu.VMEM((width, 2 * inner + channels), BF16),
            pltpu.VMEM((blocks, 2 * tok, width), BF16),
            pltpu.VMEM((blocks, 2 * tok, 2 * inner), BF16),
            pltpu.VMEM((blocks, 2 * tok, 2 * channels), F32),
            pltpu.VMEM((samples, blocks, 2, tok, 2 * inner), BF16),
            pltpu.VMEM((heads * tok, total), BF16),
            pltpu.VMEM((samples * tok, width), F32),
            pltpu.VMEM((samples * tok, width), F32),
            pltpu.VMEM((inner, width), BF16),
            pltpu.VMEM((width, channels), BF16),
            pltpu.VMEM((2, rows, total), F32),
            pltpu.VMEM((samples, 2, rows, total), BF16),
            pltpu.VMEM((samples, 2, rows, 256), F32),
            pltpu.VMEM((samples, 2, rows, 128), F32),
            pltpu.VMEM((samples * tok, inner), BF16),
            pltpu.VMEM((samples * tok, inner), BF16),
            pltpu.SemaphoreType.DMA((13,)),
        ],
        compiler_params=params(),
        name="attend",
    )(
        place,
        pooled_z,
        pooled_y,
        w_mix,
        w_big,
        got_t,
        tokens_in,
        queries,
        d_normed,
        w_out_all,
        w_down_all,
        pair_bias.reshape(heads * tok, total),
    )

    other = lax.ppermute(send, "samp", swap)
    both = (keep.astype(F32) + other.astype(F32)).astype(BF16)
    shares = lax.all_to_all(both, "samp", 0, 0, axis_index_groups=sets, tiled=True)
    bias_grad = jnp.sum(shares.astype(F32), axis=0).reshape(heads, tok, 128)

    proj = proj.reshape(samples, tok, channels)
    proj_left = lax.ppermute(proj[:, margin:], "rows", up)
    proj_right = lax.ppermute(proj[:, :margin], "rows", down)
    atom_out = pl.pallas_call(
        decode_kernel,
        out_shape=shape((samples, atoms, channels), BF16),
        in_specs=[SCALAR] + [WHOLE] * 5,
        out_specs=WHOLE,
        compiler_params=params(),
        name="decode",
    )(atom_count, local_token[:, None], hidden, proj, proj_left, proj_right)
    return (atom_out, bias_grad)


def solution(mesh):
    placed = (
        P("samp", "rows", None),
        P("rows", None),
        P("rows"),
        P("rows"),
        P("rows", None),
        P(None, "rows", None),
        P(),
        P("samp", None),
        P("samp", None),
        P("samp", None),
        P("samp", None),
        P("samp", None),
        P("samp", None),
        P("samp", "rows", None),
    )
    return jax.shard_map(
        local,
        mesh=mesh,
        in_specs=placed,
        out_specs=(P("samp", "rows", None), P(None, "rows", "samp")),
        check_vma=False,
    )
```

```python
import functools

import jax
import jax.numpy as jnp
from jax import lax
from jax.experimental import pallas as pl
from jax.experimental.pallas import tpu as pltpu
from jax.sharding import PartitionSpec as P

EPSILON = 1e-05
F32 = jnp.float32
BF16 = jnp.bfloat16
VMEM_BYTES = 56 * 1024 * 1024
WHOLE = pl.BlockSpec(memory_space=pltpu.VMEM)
SCALAR = pl.BlockSpec(memory_space=pltpu.SMEM)
ANY = pl.BlockSpec(memory_space=pl.ANY)


def dot(left, right):
    return lax.dot_general(left, right, (((1,), (0,)), ((), ())), preferred_element_type=F32)


def dot_nt(left, right):
    return lax.dot_general(left, right, (((1,), (1,)), ((), ())), preferred_element_type=F32)


def params():
    return pltpu.CompilerParams(vmem_limit_bytes=VMEM_BYTES)


def normalize(values):
    average = jnp.mean(values, axis=-1, keepdims=True)
    centered = values - average
    variance = jnp.mean(centered * centered, axis=-1, keepdims=True)
    inverse = lax.rsqrt(variance + EPSILON)
    return centered * inverse, inverse


def pool_kernel(count, token, noised, single, w_atom, d_out, hidden, own, left, right):
    samples, atoms, channels = noised.shape
    wide = own.shape[1] + left.shape[1] + right.shape[1]
    margin = left.shape[1]
    middle = own.shape[1]
    slot = lax.broadcasted_iota(jnp.int32, (wide, atoms), 1)
    line = lax.broadcasted_iota(jnp.int32, (wide, atoms), 0)
    picked = (line == token[...]) & (slot < count[0])
    one_hot = jnp.where(picked, 1.0, 0.0).astype(BF16)

    def put(index, sums):
        left[index] = sums[:margin]
        own[index] = sums[margin : margin + middle]
        right[index] = sums[margin + middle :]

    single_f = single[...].astype(F32)
    for s in range(samples):
        query = (noised[s].astype(F32) + single_f).astype(BF16)
        pre = dot(query, w_atom[...])
        value = (query.astype(F32) + pre / (1.0 + jnp.exp(-pre))).astype(BF16)
        hidden[s] = value
        put(s, dot(one_hot, value))
    put(samples, dot(one_hot, jnp.ones((atoms, channels), BF16)))
    for s in range(samples):
        put(samples + 1 + s, dot(one_hot, d_out[s]))


def settle_kernel(own, from_left, from_right, pooled, d_token):
    margin = from_left.shape[1]
    samples = (own.shape[0] - 1) // 2
    middle = own.shape[1]

    def settled(index):
        return jnp.concatenate(
            [own[index, :margin] + from_left[index], own[index, margin:] + from_right[index]], axis=0
        )

    scale = 1.0 / jnp.maximum(settled(samples), 1.0)
    for s in range(samples):
        pooled[s * middle : (s + 1) * middle] = (settled(s) * scale).astype(BF16)
        d_token[s * middle : (s + 1) * middle] = settled(samples + 1 + s).astype(BF16)


def pack_kernel(w_query, w_key, w_value, w_down, w_out, w_up, out):
    cut, inner = w_query.shape
    channels = w_down.shape[1]
    out[:cut, :inner] = w_query[...]
    out[:cut, inner:] = w_key[...]
    value = w_value[...].astype(F32)
    down = w_down[...].astype(F32)
    piece = cut * channels // out.shape[1]
    rest = [
        jnp.concatenate([value[: cut // 2], value[cut // 2 :]], axis=1),
        w_out[...].astype(F32),
        jnp.concatenate([down[i : i + piece] for i in range(0, cut, piece)], axis=1),
        w_up[...].astype(F32),
    ]
    out[cut:] = jnp.concatenate(rest, axis=0).astype(BF16)


def prep_kernel(
    head_dim, got, pooled, d_token, t_own, w_big, w_mix, tokens_in, queries, d_normed, w_out, w_down
):
    members, height, width = got.shape
    tok = t_own.shape[0]
    channels = pooled.shape[1]
    samples = pooled.shape[0] // tok
    inner = queries.shape[1]
    cut = width // members
    half = cut // 2
    out_rows = inner // members
    piece = cut * channels // width

    rest = got[:, cut:, :].astype(F32)
    value = jnp.concatenate([rest[:, :half, :inner], rest[:, :half, inner:]], axis=1).reshape(width, inner)
    at = half + out_rows
    w_out[...] = rest[:, half:at].reshape(inner, width).astype(BF16)
    down = [rest[:, at : at + piece, i : i + channels] for i in range(0, width, channels)]
    w_down[...] = jnp.concatenate(down, axis=1).reshape(width, channels).astype(BF16)
    up_exact = rest[:, at + piece :].reshape(channels, width)
    up = (up_exact - jnp.mean(up_exact, axis=-1, keepdims=True)).astype(BF16)
    w_big[:, :inner] = got[:, :cut, inner:].reshape(width, inner)
    w_big[:, inner : 2 * inner] = value.astype(BF16)
    w_big[:, 2 * inner :] = up.astype(F32).T.astype(BF16)
    mix = dot(up, w_big[...])
    w_mix[:, : 2 * inner] = mix[:, : 2 * inner].astype(BF16)
    gram = mix[:, 2 * inner :] * (1.0 / width)
    high = gram.astype(BF16)
    w_mix[:, 2 * inner : 2 * inner + channels] = high
    w_mix[:, 2 * inner + channels :] = (gram - high.astype(F32)).astype(BF16)

    w_query = got[:, :cut, :inner].reshape(width, inner)
    t_f = t_own[...].astype(F32)
    for s in range(samples):
        own_rows = slice(s * tok, (s + 1) * tok)
        tokens_in[own_rows] = dot(pooled[own_rows], up_exact.astype(BF16)) + t_f
    normed, _ = normalize(tokens_in[...])
    queries[...] = (dot(normed.astype(BF16), w_query) * (head_dim**-0.5)).astype(BF16)
    d_normed[...] = dot_nt(d_token[...], w_down[...])


def attend_kernel(
    heads,
    factor,
    place,
    pooled_z,
    pooled_y,
    w_mix,
    w_big_hbm,
    got_t,
    tokens_hbm,
    queries,
    d_normed_hbm,
    w_out_hbm,
    w_down_hbm,
    bias_hbm,
    proj,
    keep,
    send,
    w_big,
    t_all,
    base,
    extra,
    kv,
    bias,
    tokens_in,
    d_normed,
    w_out,
    w_down,
    scores,
    probs,
    mixed_full,
    inv_sum,
    mixed,
    d_mixed,
    sems,
):
    blocks, lines, channels = pooled_y.shape
    samples, _, _, tok, deep = kv.shape
    width = tokens_in.shape[1]
    total = 2 * blocks * tok
    inner = deep // 2
    head_dim = inner // heads
    half = heads // 2
    rows = half * tok
    span = 256
    starts = (0, inner - span)
    first_z = place[0]
    high = place[1]
    core = place[2]
    pieces_in = min(4, blocks // 2)
    run = blocks // pieces_in

    def copy(src, dst, index):
        made = pltpu.make_async_copy(src, dst, sems.at[index])
        made.start()
        return made

    big_copy = copy(w_big_hbm, w_big, 8)
    copies = []
    for piece in range(pieces_in):
        part = pl.ds(piece * run, run)
        copies.append(copy(got_t.at[part], t_all.at[part], piece))
    late = [
        copy(bias_hbm, bias, 7),
        copy(tokens_hbm, tokens_in, 9),
        copy(d_normed_hbm, d_normed, 10),
        copy(w_out_hbm, w_out, 11),
        copy(w_down_hbm, w_down, 12),
    ]

    big_copy.wait()
    block = 2 * tok
    for piece in range(pieces_in):
        copies[piece].wait()
        part = slice(piece * run, (piece + 1) * run)
        t = t_all[part].reshape(run * block, width).astype(F32)
        cent = (t - jnp.mean(t, axis=-1, keepdims=True)).astype(BF16)
        both = dot(cent, w_big[...])
        base[part] = both[:, :deep].astype(BF16).reshape(run, block, deep)
        wide = cent.astype(F32)
        square = jnp.sum(wide * wide, axis=-1, keepdims=True) * (1.0 / width)
        extra[part, :, :channels] = (both[:, deep:] * (2.0 / width)).reshape(run, block, channels)
        extra[part, :, channels:] = jnp.broadcast_to(square, (run * block, channels)).reshape(run, block, channels)

    def step(b, carry):
        near = lax.rem(first_z + b, blocks)
        far = lax.rem(near + high, blocks)
        p = jnp.concatenate([pooled_z[near], pooled_y[far]], axis=0)
        pf = p.astype(F32)
        gram = dot(p, w_mix[:, deep:])
        inverse = []
        for part in range(2):
            own = slice(part * tok, (part + 1) * tok)
            cross = extra[b, own, :channels]
            square = extra[b, own, channels:]
            for s in range(samples):
                lane = slice(part * lines + s * tok, part * lines + (s + 1) * tok)
                form = pf[lane] * (gram[lane, :channels] + gram[lane, channels:] + cross)
                variance = jnp.sum(form, axis=-1, keepdims=True) + square[:, :1]
                inverse.append(lax.rsqrt(jnp.maximum(variance, 0.0) + EPSILON))
        for c in range(0, deep, span):
            y = dot(p, w_mix[:, c : c + span])
            for part, (z, y_half) in enumerate(((near, high), (far, 1 - high))):
                shared = base[b, part * tok : (part + 1) * tok, c : c + span].astype(F32)
                for s in range(samples):
                    lane = slice(part * lines + s * tok, part * lines + (s + 1) * tok)
                    kv[s, z, y_half, :, c : c + span] = (
                        (y[lane] + shared) * inverse[part * samples + s]
                    ).astype(BF16)
        return carry

    lax.fori_loop(0, blocks // 2, lambda i, c: step(2 * i + 1, step(2 * i, c)), 0)
    for made in late:
        made.wait()

    lane_head = lax.broadcasted_iota(jnp.int32, (rows, span), 1)
    row_head = lax.broadcasted_iota(jnp.int32, (rows, span), 0) // tok

    def head_mask(g):
        lo = (row_head + g * half) * head_dim - starts[g]
        return (lane_head >= lo) & (lane_head < lo + head_dim)

    def spread(values, g):
        tile = values[:, starts[g] : starts[g] + span].astype(F32)
        return jnp.where(head_mask(g), jnp.concatenate([tile] * half, axis=0), 0.0)

    chunk = 512

    def keys(s, start, count, lanes):
        return kv[s, pl.ds(start // (2 * tok), count // (2 * tok)), :, :, lanes].reshape(count, span)

    def forward(s, carry):
        own_rows = pl.ds(pl.multiple_of(s * tok, tok), tok)
        pieces = []
        for g in range(2):
            q = spread(queries[own_rows, :], g).astype(BF16)
            lanes = slice(starts[g], starts[g] + span)
            value_lanes = slice(inner + starts[g], inner + starts[g] + span)
            top = jnp.full((rows, 128), -jnp.inf, F32)
            for j in range(0, total, span):
                part = dot_nt(q, keys(s, j, span, lanes))
                part = part + bias[g * rows : (g + 1) * rows, j : j + span].astype(F32)
                scores[g, :, j : j + span] = part
                for c in range(0, span, 128):
                    top = jnp.maximum(top, part[:, c : c + 128])
            top = jnp.max(top, axis=-1, keepdims=True)
            amount = jnp.zeros((rows, 128), F32)
            out = jnp.zeros((rows, span), F32)
            for j in range(0, total, chunk):
                e = jnp.exp(scores[g, :, j : j + chunk] - top)
                for c in range(0, chunk, 128):
                    amount = amount + e[:, c : c + 128]
                e = e.astype(BF16)
                probs[s, g, :, j : j + chunk] = e
                out = out + dot(e, keys(s, j, chunk, value_lanes))
            inverse = 1.0 / jnp.sum(amount, axis=-1, keepdims=True)
            out = jnp.where(head_mask(g), out * inverse, 0.0)
            mixed_full[s, g] = out
            inv_sum[s, g] = jnp.broadcast_to(inverse, (rows, 128))
            piece = out[:tok]
            for h in range(1, half):
                piece = piece + out[h * tok : (h + 1) * tok]
            pieces.append(piece)
        cut = starts[1]
        mixed[own_rows, :cut] = pieces[0][:, :cut].astype(BF16)
        mixed[own_rows, cut:span] = (pieces[0][:, cut:] + pieces[1][:, : span - cut]).astype(BF16)
        mixed[own_rows, span:] = pieces[1][:, span - cut :].astype(BF16)
        return carry

    lax.fori_loop(0, samples, forward, 0)

    normed_out, inverse_out = normalize(tokens_in[...] + dot(mixed[...], w_out[...]))
    proj[...] = dot(normed_out.astype(BF16), w_down[...]).astype(BF16)
    d_norm = d_normed[...]
    first = jnp.mean(d_norm, axis=-1, keepdims=True)
    second = jnp.mean(d_norm * normed_out, axis=-1, keepdims=True)
    d_tokens = inverse_out * (d_norm - first - normed_out * second)
    d_mixed[...] = dot_nt(d_tokens.astype(BF16), w_out[...]).astype(BF16)

    for g in range(2):
        value_lanes = slice(inner + starts[g], inner + starts[g] + span)
        wide = []
        delta = []
        scale = []
        for s in range(samples):
            w = spread(d_mixed[s * tok : (s + 1) * tok, :], g)
            wide.append(w.astype(BF16))
            delta.append(jnp.sum(w * mixed_full[s, g], axis=-1, keepdims=True))
            scale.append(inv_sum[s, g][:, :1] * factor)

        def backward(k, carry):
            cols = pl.ds(pl.multiple_of(k * 256, 256), 256)
            grad = None
            for s in range(samples):
                d_prob = dot_nt(wide[s], keys(s, k * 256, 256, value_lanes))
                term = probs[s, g, :, cols].astype(F32) * ((d_prob - delta[s]) * scale[s])
                grad = term if grad is None else grad + term
            low = grad[:, :128]
            high = grad[:, 128:]
            keep[k, g * rows : (g + 1) * rows, :] = jnp.where(core == 0, low, high).astype(BF16)
            send[k, g * rows : (g + 1) * rows, :] = jnp.where(core == 0, high, low).astype(BF16)
            return carry

        lax.fori_loop(0, total // 512, lambda i, c: backward(2 * i + 1, backward(2 * i, c)), 0)


def decode_kernel(count, token, hidden, proj, from_left, from_right, out):
    samples, atoms, channels = hidden.shape
    tok = proj.shape[1]
    wide = tok + 2 * from_left.shape[1]
    line = lax.broadcasted_iota(jnp.int32, (atoms, wide), 1)
    one_hot = jnp.where(line == token[...], 1.0, 0.0).astype(BF16)
    alive = lax.broadcasted_iota(jnp.int32, (atoms, channels), 0) < count[0]
    for s in range(samples):
        table = jnp.concatenate([from_left[s], proj[s], from_right[s]], axis=0)
        value = hidden[s].astype(F32) + dot(one_hot, table)
        out[s] = jnp.where(alive, value, 0.0).astype(BF16)


def local(
    atom_noised,
    atom_single,
    atom_token,
    atom_count,
    token_single,
    pair_bias,
    w_atom,
    w_up,
    w_query,
    w_key,
    w_value,
    w_out,
    w_down,
    d_atom_out,
):
    samples, atoms, channels = atom_noised.shape
    tok, width = token_single.shape
    margin = tok // 2
    heads, _, total = pair_bias.shape
    n_rows = lax.axis_size("rows")
    n_samp = lax.axis_size("samp")
    inner = w_query.shape[1]
    rank = lax.axis_index("rows")
    group = lax.axis_index("samp")
    chips = n_samp // 2

    blocks = n_rows // 2
    sets = [[2 * m + c for m in range(chips)] for c in range(2)]
    swap = [(s, s ^ 1) for s in range(n_samp)]

    shape = jax.ShapeDtypeStruct
    packed = sum(w.size for w in (w_query, w_key, w_value, w_down, w_out, w_up))
    w_own = pl.pallas_call(
        pack_kernel,
        out_shape=shape((packed // width, width), BF16),
        in_specs=[WHOLE] * 6,
        out_specs=WHOLE,
        compiler_params=params(),
        name="pack",
    )(w_query, w_key, w_value, w_down, w_out, w_up)
    w_own, atom_noised = lax.optimization_barrier((w_own, atom_noised))
    got = lax.all_gather(w_own, "samp", axis=0, tiled=False)

    fetched = []
    for part in range(2):
        perm = [
            ((r + 2 * s + part) % n_rows * n_samp + s, r * n_samp + s)
            for r in range(n_rows)
            for s in range(n_samp)
        ]
        fetched.append(lax.ppermute(token_single, ("rows", "samp"), perm))

    local_token = atom_token - (rank * tok - margin)
    sums = 2 * samples + 1
    hidden, own, left, right = pl.pallas_call(
        pool_kernel,
        out_shape=(
            shape((samples, atoms, channels), BF16),
            shape((sums, tok, channels), F32),
            shape((sums, margin, channels), F32),
            shape((sums, margin, channels), F32),
        ),
        in_specs=[SCALAR] + [WHOLE] * 5,
        out_specs=(WHOLE,) * 4,
        compiler_params=params(),
        name="pool",
    )(atom_count, local_token[None, :], atom_noised, atom_single, w_atom, d_atom_out)
    up = [(i, i + 1) for i in range(n_rows - 1)]
    down = [(i + 1, i) for i in range(n_rows - 1)]

    from_left = lax.ppermute(right, "rows", up)
    from_right = lax.ppermute(left, "rows", down)
    pooled, d_token = pl.pallas_call(
        settle_kernel,
        out_shape=(shape((samples * tok, channels), BF16), shape((samples * tok, channels), BF16)),
        in_specs=[WHOLE] * 3,
        out_specs=(WHOLE,) * 2,
        compiler_params=params(),
        name="settle",
    )(own, from_left, from_right)
    fetched[0], fetched[1], pooled = lax.optimization_barrier((fetched[0], fetched[1], pooled))
    t_own_pair = jnp.concatenate(fetched, axis=0)
    pooled, t_own_pair = lax.optimization_barrier((pooled, t_own_pair))
    got_t = lax.all_gather(t_own_pair, "samp", axis=0, tiled=False)
    z_sets = [[2 * z + y for z in range(n_rows // 2)] for y in range(2)]
    pooled_z = lax.all_gather(pooled, "rows", axis=0, tiled=False, axis_index_groups=z_sets)
    pooled_y = lax.ppermute(pooled_z, "rows", [(r, r ^ 1) for r in range(n_rows)])

    got_t, pooled_y = lax.optimization_barrier((got_t, pooled_y))

    place = jnp.stack([rank // 2, rank % 2, group % 2]).astype(jnp.int32)
    w_big, w_mix, tokens_in, queries, d_normed, w_out_all, w_down_all = pl.pallas_call(
        functools.partial(prep_kernel, inner // heads),
        out_shape=(
            shape((width, 2 * inner + channels), BF16),
            shape((channels, 2 * inner + 2 * channels), BF16),
            shape((samples * tok, width), F32),
            shape((samples * tok, inner), BF16),
            shape((samples * tok, width), F32),
            shape((inner, width), BF16),
            shape((width, channels), BF16),
        ),
        in_specs=[WHOLE] * 4,
        out_specs=(WHOLE,) * 7,
        compiler_params=params(),
        cost_estimate=pl.CostEstimate(flops=2 * 10**9, bytes_accessed=8 * 10**6, transcendentals=0),
        name="prep",
    )(got, pooled, d_token, token_single)

    factor = total / (samples * n_samp)
    rows = heads // 2 * tok
    proj, keep, send = pl.pallas_call(
        functools.partial(attend_kernel, heads, factor),
        out_shape=(
            shape((samples * tok, channels), BF16),
            shape((chips, heads * tok, 128), BF16),
            shape((chips, heads * tok, 128), BF16),
        ),
        in_specs=[SCALAR, WHOLE, WHOLE, WHOLE, ANY, ANY, ANY, WHOLE, ANY, ANY, ANY, ANY],
        out_specs=(WHOLE,) * 3,
        scratch_shapes=[
            pltpu.VMEM((width, 2 * inner + channels), BF16),
            pltpu.VMEM((blocks, 2 * tok, width), BF16),
            pltpu.VMEM((blocks, 2 * tok, 2 * inner), BF16),
            pltpu.VMEM((blocks, 2 * tok, 2 * channels), F32),
            pltpu.VMEM((samples, blocks, 2, tok, 2 * inner), BF16),
            pltpu.VMEM((heads * tok, total), BF16),
            pltpu.VMEM((samples * tok, width), F32),
            pltpu.VMEM((samples * tok, width), F32),
            pltpu.VMEM((inner, width), BF16),
            pltpu.VMEM((width, channels), BF16),
            pltpu.VMEM((2, rows, total), F32),
            pltpu.VMEM((samples, 2, rows, total), BF16),
            pltpu.VMEM((samples, 2, rows, 256), F32),
            pltpu.VMEM((samples, 2, rows, 128), F32),
            pltpu.VMEM((samples * tok, inner), BF16),
            pltpu.VMEM((samples * tok, inner), BF16),
            pltpu.SemaphoreType.DMA((13,)),
        ],
        compiler_params=params(),
        name="attend",
    )(
        place,
        pooled_z,
        pooled_y,
        w_mix,
        w_big,
        got_t,
        tokens_in,
        queries,
        d_normed,
        w_out_all,
        w_down_all,
        pair_bias.reshape(heads * tok, total),
    )

    other = lax.ppermute(send, "samp", swap)
    both = (keep.astype(F32) + other.astype(F32)).astype(BF16)
    shares = lax.all_to_all(both, "samp", 0, 0, axis_index_groups=sets, tiled=True)
    bias_grad = jnp.sum(shares.astype(F32), axis=0).reshape(heads, tok, 128)

    proj = proj.reshape(samples, tok, channels)
    proj_left = lax.ppermute(proj[:, margin:], "rows", up)
    proj_right = lax.ppermute(proj[:, :margin], "rows", down)
    atom_out = pl.pallas_call(
        decode_kernel,
        out_shape=shape((samples, atoms, channels), BF16),
        in_specs=[SCALAR] + [WHOLE] * 5,
        out_specs=WHOLE,
        compiler_params=params(),
        name="decode",
    )(atom_count, local_token[:, None], hidden, proj, proj_left, proj_right)
    return (atom_out, bias_grad)


def solution(mesh):
    placed = (
        P("samp", "rows", None),
        P("rows", None),
        P("rows"),
        P("rows"),
        P("rows", None),
        P(None, "rows", None),
        P(),
        P("samp", None),
        P("samp", None),
        P("samp", None),
        P("samp", None),
        P("samp", None),
        P("samp", None),
        P("samp", "rows", None),
    )
    return jax.shard_map(
        local,
        mesh=mesh,
        in_specs=placed,
        out_specs=(P("samp", "rows", None), P(None, "rows", "samp")),
        check_vma=False,
    )
```
